32 devices in a mesh: gx: 8 (over y, x, core), gy: 4 (over z).
Axes of the slice: x: 2, y: 2, z: 4, core: 2. Of those that a mesh axis runs over, the one named last changes fastest.
Arguments:
- density: float32 [512, 2048], P('gx', 'gy'), may hold values from 0.5 to 4
- energy: float32 [512, 2048], P('gx', 'gy'), may hold values from 0.5 to 3
- displacement: float32 [2, 512, 2048], P(None, 'gx', 'gy'), may hold values from -0.4 to 0.4
- tile_mat: int32 [512, 16], P('gx', 'gy'), may hold values from 0 to 3
- store_frac: float32 [1024, 128], P(('gx', 'gy')), may hold values from 0.05 to 0.95
- store_state: float32 [2, 1024, 128], P(None, ('gx', 'gy')), may hold values from 0.5 to 4
- store_route: int32 [3, 1024], P(None, ('gx', 'gy')), may hold values from 0 to 255, as said below
Outputs:
- remapped: float32 [4, 3, 512, 2048], P(None, None, 'gx', 'gy')
- totals: float32 [2, 4], replicated
The draws below stay inside these ranges and needn't reach their ends.
Inputs may be any that keep to these rules, and one draw needn't show every extreme that they name: `store_route`: row 0 is an index along gy; among the stored tiles of one device at most 16 have the same row-0 value, and in every draw some device reaches 16 for some value. Row 1 is a tile index of 0 to 255; stored tiles with the same receiving device (same gx block row, same row-0 value) name distinct tiles. Row 2 is a material of 0 to 3 that differs from tile_mat of the named tile.
All inputs are finite; a program needn't handle non-finite values.
Results may differ from the reference program's by a relative error of at most 0.0003.
Values sent between devices are 32-bit elements; how exact they have to be, the bound alone decides.
A program may use at most 64 MiB of HBM per device.

```python
import math
import jax
import jax.numpy as jnp
from jax import lax

M = 4
TILE = 128
CX = 64
CY = 512
CAP = 16
SLOTS = 32
STORE = 1024
NX = 512
NY = 2048
N_GX = 8
N_GY = 4


def layout(base_key):
    key_list = jax.random.split(jax.random.fold_in(base_key, 7), 7)
    block_count = N_GX * N_GY
    virtual_count = N_GY * CAP
    per_row = CY // TILE
    tile_total = CX * per_row
    tile_map = jax.random.randint(key_list[0], (NX, NY // TILE), 0, M).astype(jnp.int32)
    jitter = jax.random.randint(key_list[1], (block_count, virtual_count), 0, 256)
    common = jax.random.randint(key_list[2], (N_GY,), 0, 2048)
    private = jax.random.randint(key_list[3], (block_count, N_GY), 0, 512)
    forced = jax.random.randint(key_list[4], (block_count,), 0, N_GY)
    virtual = jnp.arange(virtual_count, dtype=jnp.int32)
    virtual_gy = virtual // CAP
    weight_gy = common[None, :] + private
    weight_slot = weight_gy[:, virtual_gy]
    weight_slot = jnp.where(virtual_gy[None, :] == forced[:, None], -1, weight_slot)
    scores = ((weight_slot + 1) * 256 + jitter) * virtual_count + virtual[None, :]
    chosen = jnp.argsort(scores, axis=1)[:, :SLOTS]
    row_targets = (chosen // CAP).astype(jnp.int32).reshape(N_GX, N_GY * SLOTS)
    onehot = (row_targets[:, :, None] == jnp.arange(N_GY, dtype=jnp.int32)[None, None, :]).astype(jnp.int32)
    rank = jnp.sum((jnp.cumsum(onehot, 1) - onehot) * onehot, 2)
    tile_scores = jax.random.randint(key_list[5], (N_GX, N_GY, tile_total), 0, 65536) * tile_total
    tile_scores = tile_scores + jnp.arange(tile_total, dtype=jnp.int32)[None, None, :]
    orders = jnp.argsort(tile_scores, axis=2).astype(jnp.int32)
    gx_of_row = jnp.arange(N_GX, dtype=jnp.int32)[:, None]
    target_tile = orders[gx_of_row, row_targets, rank]
    tile_row = gx_of_row * CX + target_tile // per_row
    tile_column = row_targets * per_row + target_tile % per_row
    primary = tile_map[tile_row, tile_column]
    offset = jax.random.randint(key_list[6], primary.shape, 1, M)
    second = ((primary + offset) % M).astype(jnp.int32)
    route = jnp.stack([row_targets, target_tile, second]).reshape(3, STORE).astype(jnp.int32)
    return (tile_map, route)


def draw_tile_mat(key, part):
    return layout(key)[0]


def draw_store_route(key, part):
    return layout(key)[1]


def level_of(key, extent, cuts, least, top_value):
    gain = 1.0
    for axis_at, shards_of in cuts:
        steps = jax.random.uniform(jax.random.fold_in(jax.random.fold_in(key, 6), axis_at), (shards_of,), jnp.float32, least / len(cuts), top_value / len(cuts))
        gain = gain * jnp.repeat(jnp.exp(steps), extent[axis_at] // shards_of).reshape((-1,) + (1,) * (len(extent) - 1 - axis_at))
    return gain


def setup_inputs(seed: int = 0) -> dict:
    key_of = jax.random.split(jax.random.key(seed), 8)
    return {
        "density": jnp.clip(jnp.exp(math.log(4.0) - 2.0794415 * jax.random.uniform(key_of[0], (NX, NY), jnp.float32) ** level_of(key_of[0], (NX, NY), ((0, 8), (1, 4)), -0.2, 0.2)), 0.5, 4.0),
        "energy": jnp.clip(jnp.exp(math.log(3.0) - 1.7917595 * jax.random.uniform(key_of[1], (NX, NY), jnp.float32) ** level_of(key_of[1], (NX, NY), ((0, 8), (1, 4)), -0.2, 0.2)), 0.5, 3.0),
        "displacement": jnp.clip(jax.random.uniform(key_of[2], (2, NX, NY), jnp.float32, -0.4, 0.4) * level_of(key_of[2], (2, NX, NY), ((1, 8), (2, 4)), -0.4, 0.0), -0.4, 0.4),
        "tile_mat": draw_tile_mat(jax.random.fold_in(key_of[7], 71), 0),
        "store_frac": jnp.clip(0.05 + 0.9 * jax.random.uniform(key_of[4], (STORE, TILE), jnp.float32) ** level_of(key_of[4], (STORE, TILE), ((0, 32),), -0.2, 0.2), 0.05, 0.95),
        "store_state": jnp.clip(jnp.exp(math.log(4.0) - 2.0794415 * jax.random.uniform(key_of[5], (2, STORE, TILE), jnp.float32) ** level_of(key_of[5], (2, STORE, TILE), ((1, 32),), -0.2, 0.2)), 0.5, 4.0),
        "store_route": draw_store_route(jax.random.fold_in(key_of[7], 71), 0),
    }


def slopes(padded):
    across_sum = padded[..., :, :-2] + padded[..., :, 1:-1] + padded[..., :, 2:]
    slope_x = (across_sum[..., 2:, :] - across_sum[..., :-2, :]) / 6.0
    along_sum = padded[..., :-2, :] + padded[..., 1:-1, :] + padded[..., 2:, :]
    slope_y = (along_sum[..., :, 2:] - along_sum[..., :, :-2]) / 6.0
    return slope_x, slope_y


def upwind(face_speed, lower_side, upper_side):
    return face_speed * 0.5 * (lower_side + upper_side) - 0.5 * jnp.abs(face_speed) * (upper_side - lower_side)


def advance(extended, slope_x, slope_y, x_speed, y_speed):
    lower_side = extended[..., :-1, 1:-1] + 0.5 * slope_x[..., :-1, 1:-1]
    upper_side = extended[..., 1:, 1:-1] - 0.5 * slope_x[..., 1:, 1:-1]
    x_flux = upwind(x_speed, lower_side, upper_side)
    left_side = extended[..., 1:-1, :-1] + 0.5 * slope_y[..., 1:-1, :-1]
    right_side = extended[..., 1:-1, 1:] - 0.5 * slope_y[..., 1:-1, 1:]
    y_flux = upwind(y_speed, left_side, right_side)
    interior = extended[..., 1:-1, 1:-1]
    return interior + x_flux[..., :-1, :] - x_flux[..., 1:, :] + y_flux[..., :, :-1] - y_flux[..., :, 1:]


def speeds(node_disp, x_open, y_open):
    x_speed = -0.5 * (node_disp[0, :, :-1] + node_disp[0, :, 1:])
    y_speed = -0.5 * (node_disp[1, :-1, :] + node_disp[1, 1:, :])
    return x_speed * x_open[:, None], y_speed * y_open[None, :]


def conserved(primary, second, mixed_data, density, energy, material):
    own_part = (primary == material).astype(jnp.float32) * (1.0 - mixed_data[0])
    other_part = (second == material).astype(jnp.float32) * mixed_data[0]
    volume = own_part + other_part
    mass = own_part * density + other_part * mixed_data[1]
    energy_total = own_part * density * energy + other_part * mixed_data[1] * mixed_data[2]
    return jnp.stack([volume, mass, energy_total])


def reference(density, energy, displacement, tile_mat, store_frac, store_state, store_route):
    per_row = CY // TILE
    slot_index = jnp.arange(STORE, dtype=jnp.int32)
    sender_gx = slot_index // SLOTS // N_GY
    tile_row = sender_gx * CX + store_route[1] // per_row
    tile_column = store_route[0] * per_row + store_route[1] % per_row
    payload = jnp.stack([store_frac, store_state[0], store_state[1]])
    mixed_data = jnp.zeros((3, NX, NY // TILE, TILE), jnp.float32).at[:, tile_row, tile_column].set(payload)
    mixed_data = mixed_data.reshape(3, NX, NY)
    second = jnp.full((NX, NY // TILE), -1, jnp.int32).at[tile_row, tile_column].set(store_route[2])
    second = jnp.repeat(second, TILE, axis=1)
    primary = jnp.repeat(tile_mat, TILE, axis=1)
    node_disp = jnp.pad(displacement, ((0, 0), (0, 1), (0, 1)))
    x_open = jnp.ones((NX + 1,), jnp.float32).at[0].set(0.0).at[NX].set(0.0)
    y_open = jnp.ones((NY + 1,), jnp.float32).at[0].set(0.0).at[NY].set(0.0)
    x_speed, y_speed = speeds(node_disp, x_open, y_open)

    def one_material(material):
        fields = conserved(primary, second, mixed_data, density, energy, material)
        padded = jnp.pad(fields, ((0, 0), (2, 2), (2, 2)))
        slope_x, slope_y = slopes(padded)
        return advance(padded[:, 1:-1, 1:-1], slope_x, slope_y, x_speed, y_speed)

    remapped = lax.map(one_material, jnp.arange(M, dtype=jnp.int32))
    totals = jnp.sum(remapped[:, 1:], axis=(2, 3)).T
    return remapped, totals
```

```python
import functools
import jax
import jax.numpy as jnp
from jax import lax
from jax.experimental import pallas as pl
from jax.experimental.pallas import tpu as pltpu
from jax.sharding import PartitionSpec as P

M = 4
F = 3 * M
TILE = 128
MESH = pl.DeviceIdType.MESH
f32 = jnp.float32
bf16 = jnp.bfloat16
NT = (((1,), (1,)), ((), ()))


def iota(shape, dim):
    return lax.broadcasted_iota(jnp.int32, shape, dim)


def split3(x):
    hi = x.astype(bf16)
    rest = x - hi.astype(f32)
    mid = rest.astype(bf16)
    low = (rest - mid.astype(f32)).astype(bf16)
    return hi, mid, low


def pick(onehot, data):
    parts = split3(data)
    o = onehot.astype(bf16)
    total = jnp.dot(o, parts[2], preferred_element_type=f32)
    total = total + jnp.dot(o, parts[1], preferred_element_type=f32)
    return total + jnp.dot(o, parts[0], preferred_element_type=f32)


def kernel(
    ngx, ngy, cap,
    density, energy, disp, tile_mat, frac, state, route,
    out, totals,
    send1, got1, drow, drow_in, dcol, dcol_in, de, ax, bx, ay, by,
    q, pk, xs, cols_in, rows_in, part, tot_y, tot_x, tot_sum,
    s1, r1, s2, r2, s3, r3, sy, ry, sx, rx,
):
    gx, gy = lax.axis_index("gx"), lax.axis_index("gy")
    rows, width = density.shape
    ext = width + TILE
    full = rows + 16
    per_row = width // TILE
    slots = frac.shape[0]
    up, down = gx > 0, gx < ngx - 1
    left, right = gy > 0, gy < ngy - 1

    def exists(dx, dy):
        ok = True
        if dx:
            ok = up if dx < 0 else down
        if dy:
            side = left if dy < 0 else right
            ok = side if ok is True else jnp.logical_and(ok, side)
        return ok

    barrier = pltpu.get_barrier_semaphore()
    diagonals = [(-1, -1), (-1, 1), (1, -1), (1, 1)]
    for k in range(1, ngy):
        pl.semaphore_signal(barrier, inc=1, device_id=(gx, lax.rem(gy + k, ngy)), device_id_type=MESH)
    for k in range(1, ngx):
        pl.semaphore_signal(barrier, inc=1, device_id=(lax.rem(gx + k, ngx), gy), device_id_type=MESH)
    for dx, dy in diagonals:
        @pl.when(exists(dx, dy))
        def _(dx=dx, dy=dy):
            pl.semaphore_signal(barrier, inc=1, device_id=(gx + dx, gy + dy), device_id_type=MESH)

    count = ngy * cap
    target = route[0:1, :]
    row = iota((count, slots), 0)
    wanted = lax.rem(gy + row // cap, ngy)
    member = (jnp.broadcast_to(target, (count, slots)) == wanted).astype(f32)
    before = (iota((slots, slots), 0) < iota((slots, slots), 1)).astype(bf16)
    rank = jnp.dot(member.astype(bf16), before, preferred_element_type=f32)
    chosen = jnp.where(rank == (row % cap).astype(f32), member, 0.0)
    payload = jnp.concatenate([frac[...], state[0], state[1]], axis=1)
    packed = pick(chosen, payload)
    named = jnp.concatenate(
        [(route[1:3, :] + 1).astype(f32), jnp.zeros((6, slots), f32)], axis=0
    )
    labels = lax.dot_general(
        named, chosen, NT, precision=lax.Precision.HIGHEST, preferred_element_type=f32
    )
    label_lane = iota((8, count), 1) // cap
    wide = send1.shape[2]
    for k in range(ngy):
        dst = got1 if k == 0 else send1
        dst[k, 0:cap, 0 : 3 * TILE] = packed[k * cap : (k + 1) * cap]
        dst[k, cap : cap + 8, 0:count] = jnp.where(label_lane == k, labels, 0.0)

    drow[...] = jnp.concatenate([disp[0, 0:8][0:1], disp[1, 0:8][0:1], jnp.zeros((6, width), f32)], axis=0)
    lane_r = iota((rows, TILE), 1)
    dcol[...] = jnp.where(lane_r == 0, disp[0, :, 0:TILE], pltpu.roll(disp[1, :, 0:TILE], 1, 1))

    diag_count = sum(exists(dx, dy).astype(jnp.int32) for dx, dy in diagonals)
    pl.semaphore_wait(barrier, ngy - 1 + ngx - 1 + diag_count)

    def remote(src, dst, s, r, to):
        return pltpu.make_async_remote_copy(
            src_ref=src, dst_ref=dst, send_sem=s, recv_sem=r, device_id=to, device_id_type=MESH
        )

    tile_copies = [
        remote(send1.at[k], got1.at[k], s1.at[k], r1.at[k], (gx, lax.rem(gy + k, ngy)))
        for k in range(1, ngy)
    ]
    for c in tile_copies:
        c.start()
    disp_moves = [
        ((-1, 0), remote(drow, drow_in, s3.at[0], r3.at[0], (gx - 1, gy))),
        ((0, -1), remote(dcol, dcol_in.at[0:rows], s3.at[1], r3.at[1], (gx, gy - 1))),
        ((-1, -1), remote(dcol.at[0:8], dcol_in.at[rows : rows + 8], s3.at[2], r3.at[2], (gx - 1, gy - 1))),
    ]
    for (dx, dy), c in disp_moves:
        @pl.when(exists(dx, dy))
        def _(c=c):
            c.start()

    @pl.when(jnp.logical_not(down))
    def _():
        drow_in[...] = jnp.zeros(drow_in.shape, f32)

    @pl.when(jnp.logical_not(right))
    def _():
        dcol_in[0:rows] = jnp.zeros((rows, TILE), f32)

    @pl.when(jnp.logical_not(exists(1, 1)))
    def _():
        dcol_in[rows : rows + 8] = jnp.zeros((8, TILE), f32)

    def row_span(dx):
        return {1: slice(0, 8), 0: slice(8, 8 + rows), -1: slice(8 + rows, full)}[dx]

    def col_span(dx):
        return {1: slice(rows - 8, rows), 0: slice(0, rows), -1: slice(0, 8)}[dx]

    def halo_copy(n, dx, dy):
        to = (gx + dx, gy + dy)
        if dy == 0:
            src, dst = xs.at[1 if dx > 0 else 0], rows_in.at[0 if dx > 0 else 1]
        else:
            src = pk.at[col_span(dx)]
            dst = cols_in.at[0 if dy > 0 else 1, row_span(dx)]
        return remote(src, dst, s2.at[n], r2.at[n], to)

    directions = [(0, 1), (0, -1)] + diagonals + [(1, 0), (-1, 0)]
    halo = [(dx, dy, halo_copy(n, dx, dy)) for n, (dx, dy) in enumerate(directions)]
    for dx, dy, _c in halo:
        @pl.when(jnp.logical_not(exists(-dx, -dy)))
        def _(dx=dx, dy=dy):
            if dy == 0:
                rows_in[0 if dx > 0 else 1] = jnp.zeros(rows_in.shape[1:], f32)
            else:
                span = row_span(dx)
                cols_in[0 if dy > 0 else 1, span] = jnp.zeros((span.stop - span.start, TILE), f32)

    zero8 = jnp.zeros((8, ext), f32)
    for f in range(F):
        q[f, 0:8] = zero8
        q[f, full - 8 : full] = zero8

    for c in tile_copies:
        c.wait_recv()
    label = got1[0, cap : cap + 8, 0:count]
    for k in range(1, ngy):
        label = label + got1[k, cap : cap + 8, 0:count]
    tiles = per_row * rows
    place = iota((tiles, count), 0)
    place = (place % rows) * per_row + place // rows + 1
    hit = (jnp.broadcast_to(label[0:1, :].astype(jnp.int32), (tiles, count)) == place).astype(f32)
    arrived = jnp.concatenate([got1[k, 0:cap, 0 : 3 * TILE] for k in range(ngy)], axis=0)
    mixed = pick(hit, arrived)
    second = jnp.dot(
        (hit * label[1:2, :]).astype(bf16), jnp.ones((count, TILE), bf16), preferred_element_type=f32
    )
    edge = []
    for c in [0] + list(range(per_row - 1, 0, -1)):
        at = slice(c * rows, (c + 1) * rows)
        lanes = slice(c * TILE, (c + 1) * TILE)
        fr, d2, e2 = (mixed[at, n * TILE : (n + 1) * TILE] for n in range(3))
        other_m = second[at]
        own_m = jnp.broadcast_to(tile_mat[:, c : c + 1], (rows, TILE))
        d1 = density[:, lanes]
        e1 = energy[:, lanes]
        de1 = d1 * e1
        de2 = d2 * e2
        clear = 1.0 - fr
        for m in range(M):
            own = jnp.where(own_m == m, clear, 0.0)
            oth = jnp.where(other_m == m + 1.0, fr, 0.0)
            for n, value in enumerate((own + oth, own * d1 + oth * d2, own * de1 + oth * de2)):
                q[3 * m + n, 8 : 8 + rows, lanes] = value
    acc = jnp.zeros((rows, TILE), f32)
    for f in range(F):
        both = jnp.where(
            lane_r < TILE // 2, q[f, 8 : 8 + rows, 0:TILE], q[f, 8 : 8 + rows, width - TILE : width]
        )
        acc = jnp.where(lane_r // 4 == f, pltpu.roll(both, 4 * f + 2, 1), acc)
    pk[...] = acc
    for dx, dy, c in halo[:6]:
        @pl.when(exists(dx, dy))
        def _(c=c):
            c.start()
    for f in range(F):
        xs[0, 2 * f : 2 * f + 2] = q[f, 8:16, 0:width][0:2]
        xs[1, 2 * f : 2 * f + 2] = q[f, rows : rows + 8, 0:width][6:8]
    for dx, dy, c in halo[6:]:
        @pl.when(exists(dx, dy))
        def _(c=c):
            c.start()

    for (dx, dy), c in disp_moves:
        @pl.when(exists(-dx, -dy))
        def _(c=c):
            c.wait_recv()
    dc = dcol_in[...]
    for c in range(2):
        de[c, 0:rows, 0:width] = disp[c]
        de[c, rows : rows + 8, 0:width] = jnp.broadcast_to(drow_in[c : c + 1, :], (8, width))
        de[c, :, width:ext] = dc if c == 0 else pltpu.roll(dc, TILE - 1, 1)
    face = iota((rows + 8, ext), 0)
    closed_x = jnp.logical_or(
        jnp.logical_and(face == 0, jnp.logical_not(up)), jnp.logical_and(face == rows, jnp.logical_not(down))
    )
    d0 = de[0]
    speed = jnp.where(closed_x, 0.0, -0.5 * (d0 + pltpu.roll(d0, ext - 1, 1)))
    ax[...] = jnp.maximum(speed, 0.0)
    bx[...] = jnp.minimum(speed, 0.0)
    face = iota((rows, ext), 1)
    closed_y = jnp.logical_or(
        jnp.logical_and(face == 0, jnp.logical_not(left)), jnp.logical_and(face == width, jnp.logical_not(right))
    )
    d1 = de[1]
    speed = jnp.where(closed_y, 0.0, -0.5 * (d1[0:rows] + pltpu.roll(d1, rows + 7, 0)[0:rows]))
    ay[...] = jnp.maximum(speed, 0.0)
    by[...] = jnp.minimum(speed, 0.0)

    for dx, dy, c in halo:
        @pl.when(exists(-dx, -dy))
        def _(c=c):
            c.wait_recv()
    lane_f = iota((full, TILE), 1)
    ring = jnp.where(lane_f % 4 < 2, cols_in[0], cols_in[1])
    for f in range(F):
        q[f, :, width:ext] = pltpu.roll(ring, TILE - 4 * f - 2, 1)
        q[f, 6:8, 0:width] = rows_in[0, 2 * f : 2 * f + 2]
        q[f, 8 + rows : 10 + rows, 0:width] = rows_in[1, 2 * f : 2 * f + 2]

    blocks = full // 8
    sub = iota((8, ext), 0)
    twelfth = 1.0 / 12.0

    def one_field(f, carry):
        qs, sums, diffs, hs, fluxes = {}, {}, {}, {}, {}

        def load(b):
            if b not in qs:
                v = q[f, b * 8 : b * 8 + 8]
                before, after = pltpu.roll(v, 1, 1), pltpu.roll(v, ext - 1, 1)
                qs[b], sums[b], diffs[b] = v, v + before + after, after - before

        def prev(values, b):
            if b == 0:
                return pltpu.roll(values[b], 1, 0)
            return pltpu.roll(jnp.where(sub == 7, values[b - 1], values[b]), 1, 0)

        def follow(values, b):
            if b == blocks - 1:
                return pltpu.roll(values[b], 7, 0)
            return pltpu.roll(jnp.where(sub == 0, values[b + 1], values[b]), 7, 0)

        low, high = {}, {}

        def sides(b):
            if b not in low:
                for n in (b - 1, b, b + 1):
                    if 0 <= n < blocks:
                        load(n)
                h = (follow(sums, b) - prev(sums, b)) * twelfth
                low[b], high[b] = qs[b] + h, qs[b] - h

        def flux(b):
            if b not in fluxes:
                sides(b - 1)
                sides(b)
                at = slice(b * 8 - 8, b * 8)
                fluxes[b] = ax[at] * prev(low, b) + bx[at] * high[b]

        total = jnp.zeros((8, width), f32)
        for b in range(1, blocks - 1):
            flux(b)
            flux(b + 1)
            at = slice(b * 8 - 8, b * 8)
            h = (diffs[b] + prev(diffs, b) + follow(diffs, b)) * twelfth
            fy = ay[at] * pltpu.roll(qs[b] + h, 1, 1) + by[at] * (qs[b] - h)
            value = qs[b] + fluxes[b] - follow(fluxes, b) + fy - pltpu.roll(fy, ext - 1, 1)
            value = value[:, 0:width]
            out[f, at] = value
            total = total + value
        lanes = total[:, 0:TILE]
        for c in range(1, per_row):
            lanes = lanes + total[:, c * TILE : (c + 1) * TILE]
        part[f] = lanes
        return carry

    lax.fori_loop(0, F, one_field, 0)

    mine = jnp.concatenate(
        [jnp.sum(part[3 * m + n], axis=0, keepdims=True) for m in range(M) for n in (1, 2)], axis=0
    )
    tot_y[gy] = mine
    copies = [
        remote(tot_y.at[gy], tot_y.at[gy], sy.at[k], ry.at[k], (gx, lax.rem(gy + k, ngy)))
        for k in range(1, ngy)
    ]
    for c in copies:
        c.start()
    incoming = [
        remote(tot_y.at[lax.rem(gy + ngy - k, ngy)], tot_y.at[lax.rem(gy + ngy - k, ngy)], sy.at[k], ry.at[k],
               (gx, lax.rem(gy + k, ngy)))
        for k in range(1, ngy)
    ]
    for c in incoming:
        c.wait_recv()
    mine = tot_y[0]
    for k in range(1, ngy):
        mine = mine + tot_y[k]
    tot_x[gx] = mine
    copies_x = [
        remote(tot_x.at[gx], tot_x.at[gx], sx.at[k], rx.at[k], (lax.rem(gx + k, ngx), gy))
        for k in range(1, ngx)
    ]
    for c in copies_x:
        c.start()
    incoming = [
        remote(tot_x.at[lax.rem(gx + ngx - k, ngx)], tot_x.at[lax.rem(gx + ngx - k, ngx)], sx.at[k], rx.at[k],
               (lax.rem(gx + k, ngx), gy))
        for k in range(1, ngx)
    ]
    for c in incoming:
        c.wait_recv()
    mine = tot_x[0]
    for k in range(1, ngx):
        mine = mine + tot_x[k]
    whole = jnp.broadcast_to(jnp.sum(mine, axis=1, keepdims=True), (2 * M, TILE))
    r8, l8 = iota((2 * M, TILE), 0), iota((2 * M, TILE), 1)
    for n in range(2):
        line = jnp.sum(jnp.where(r8 == 2 * l8 + n, whole, 0.0), axis=0, keepdims=True)
        totals[n : n + 1, :] = line[:, 0:M]

    for c in tile_copies + copies + copies_x:
        c.wait_send()
    for (dx, dy), c in disp_moves:
        @pl.when(exists(dx, dy))
        def _(c=c):
            c.wait_send()
    for dx, dy, c in halo:
        @pl.when(exists(dx, dy))
        def _(c=c):
            c.wait_send()


def local(ngx, ngy, density, energy, displacement, tile_mat, store_frac, store_state, store_route):
    rows, width = density.shape
    cap = rows * (width // TILE) // 16
    ext, full = width + TILE, rows + 16
    wide = -(-max(3 * TILE, ngy * cap) // TILE) * TILE
    vmem, dma = pltpu.VMEM, pltpu.SemaphoreType.DMA
    spec = pl.BlockSpec(memory_space=pltpu.VMEM)
    scratch = [
        vmem((ngy, cap + 8, wide), f32),
        vmem((ngy, cap + 8, wide), f32),
        vmem((8, width), f32),
        vmem((8, width), f32),
        vmem((rows, TILE), f32),
        vmem((rows + 8, TILE), f32),
        vmem((2, rows + 8, ext), f32),
        vmem((rows + 8, ext), f32),
        vmem((rows + 8, ext), f32),
        vmem((rows, ext), f32),
        vmem((rows, ext), f32),
        vmem((F, full, ext), f32),
        vmem((rows, TILE), f32),
        vmem((2, 2 * F, width), f32),
        vmem((2, full, TILE), f32),
        vmem((2, 2 * F, width), f32),
        vmem((F, 8, TILE), f32),
        vmem((ngy, 2 * M, TILE), f32),
        vmem((ngx, 2 * M, TILE), f32),
        vmem((8, TILE), f32),
        dma((ngy,)), dma((ngy,)), dma((8,)), dma((8,)), dma((3,)), dma((3,)),
        dma((ngy,)), dma((ngy,)), dma((ngx,)), dma((ngx,)),
    ]
    remapped, totals = pl.pallas_call(
        functools.partial(kernel, ngx, ngy, cap),
        out_shape=(jax.ShapeDtypeStruct((F, rows, width), f32), jax.ShapeDtypeStruct((2, M), f32)),
        in_specs=[spec] * 7,
        out_specs=(spec, spec),
        scratch_shapes=scratch,
        compiler_params=pltpu.CompilerParams(
            collective_id=0, has_side_effects=True, vmem_limit_bytes=40 * 1024 * 1024
        ),
    )(density, energy, displacement, tile_mat, store_frac, store_state, store_route)
    return remapped.reshape(M, 3, rows, width), totals


def solution(mesh):
    placed = (
        P("gx", "gy"),
        P("gx", "gy"),
        P(None, "gx", "gy"),
        P("gx", "gy"),
        P(("gx", "gy"), None),
        P(None, ("gx", "gy"), None),
        P(None, ("gx", "gy")),
    )
    return jax.shard_map(
        functools.partial(local, mesh.shape["gx"], mesh.shape["gy"]),
        mesh=mesh,
        in_specs=placed,
        out_specs=(P(None, None, "gx", "gy"), P()),
        check_vma=False,
    )
```

```python
import functools
import jax
import jax.numpy as jnp
from jax import lax
from jax.experimental import pallas as pl
from jax.experimental.pallas import tpu as pltpu
from jax.sharding import PartitionSpec as P

M = 4
F = 3 * M
TILE = 128
MESH = pl.DeviceIdType.MESH
f32 = jnp.float32
bf16 = jnp.bfloat16
NT = (((1,), (1,)), ((), ()))


def iota(shape, dim):
    return lax.broadcasted_iota(jnp.int32, shape, dim)


def split3(x):
    hi = x.astype(bf16)
    rest = x - hi.astype(f32)
    mid = rest.astype(bf16)
    low = (rest - mid.astype(f32)).astype(bf16)
    return hi, mid, low


def pick(onehot, data):
    parts = split3(data)
    o = onehot.astype(bf16)
    total = jnp.dot(o, parts[2], preferred_element_type=f32)
    total = total + jnp.dot(o, parts[1], preferred_element_type=f32)
    return total + jnp.dot(o, parts[0], preferred_element_type=f32)


def kernel(
    ngx, ngy, cap,
    density_h, energy_h, disp_h, mat_h, frac_h, state_h, route_h,
    out_h, totals,
    out, so, density, energy, disp, mat, frac, state, route, s0,
    primary, send1, got1, drow, drow_in, dcol, dcol_in, de, ax, bx, ay, by,
    q, pk, xs, cols_in, rows_in, part, tot_y, tot_x, tot_sum,
    s1, r1, s2, r2, s3, r3, sy, ry, sx, rx,
):
    gx, gy = lax.axis_index("gx"), lax.axis_index("gy")
    rows, width = density.shape
    ext = width + TILE
    full = rows + 16
    per_row = width // TILE
    slots = frac.shape[0]
    up, down = gx > 0, gx < ngx - 1
    left, right = gy > 0, gy < ngy - 1

    def exists(dx, dy):
        ok = True
        if dx:
            ok = up if dx < 0 else down
        if dy:
            side = left if dy < 0 else right
            ok = side if ok is True else jnp.logical_and(ok, side)
        return ok

    loads = [
        pltpu.make_async_copy(src, dst, s0.at[n])
        for n, (src, dst) in enumerate(
            (
                (route_h, route), (frac_h, frac), (state_h, state), (disp_h, disp),
                (mat_h, mat), (density_h, density), (energy_h, energy),
            )
        )
    ]
    for c in loads:
        c.start()

    barrier = pltpu.get_barrier_semaphore()
    diagonals = [(-1, -1), (-1, 1), (1, -1), (1, 1)]
    for k in range(1, ngy):
        pl.semaphore_signal(barrier, inc=1, device_id=(gx, lax.rem(gy + k, ngy)), device_id_type=MESH)
    for k in range(1, ngx):
        pl.semaphore_signal(barrier, inc=1, device_id=(lax.rem(gx + k, ngx), gy), device_id_type=MESH)
    for dx, dy in diagonals:
        @pl.when(exists(dx, dy))
        def _(dx=dx, dy=dy):
            pl.semaphore_signal(barrier, inc=1, device_id=(gx + dx, gy + dy), device_id_type=MESH)

    count = ngy * cap
    loads[0].wait()
    target = route[0:1, :]
    row = iota((count, slots), 0)
    wanted = lax.rem(gy + row // cap, ngy)
    member = (jnp.broadcast_to(target, (count, slots)) == wanted).astype(f32)
    before = (iota((slots, slots), 0) < iota((slots, slots), 1)).astype(bf16)
    rank = jnp.dot(member.astype(bf16), before, preferred_element_type=f32)
    chosen = jnp.where(rank == (row % cap).astype(f32), member, 0.0)
    loads[1].wait()
    loads[2].wait()
    payload = jnp.concatenate([frac[...], state[0], state[1]], axis=1)
    packed = pick(chosen, payload)
    named = jnp.concatenate(
        [(route[1:3, :] + 1).astype(f32), jnp.zeros((6, slots), f32)], axis=0
    )
    labels = lax.dot_general(
        named, chosen, NT, precision=lax.Precision.HIGHEST, preferred_element_type=f32
    )
    label_lane = iota((8, count), 1) // cap
    wide = send1.shape[2]
    for k in range(ngy):
        dst = got1 if k == 0 else send1
        dst[k, 0:cap, 0 : 3 * TILE] = packed[k * cap : (k + 1) * cap]
        dst[k, cap : cap + 8, 0:count] = jnp.where(label_lane == k, labels, 0.0)

    loads[3].wait()
    drow[...] = jnp.concatenate([disp[0, 0:8][0:1], disp[1, 0:8][0:1], jnp.zeros((6, width), f32)], axis=0)
    lane_r = iota((rows, TILE), 1)
    dcol[...] = jnp.where(lane_r == 0, disp[0, :, 0:TILE], pltpu.roll(disp[1, :, 0:TILE], 1, 1))

    diag_count = sum(exists(dx, dy).astype(jnp.int32) for dx, dy in diagonals)
    pl.semaphore_wait(barrier, ngy - 1 + ngx - 1 + diag_count)

    def remote(src, dst, s, r, to):
        return pltpu.make_async_remote_copy(
            src_ref=src, dst_ref=dst, send_sem=s, recv_sem=r, device_id=to, device_id_type=MESH
        )

    tile_copies = [
        remote(send1.at[k], got1.at[k], s1.at[k], r1.at[k], (gx, lax.rem(gy + k, ngy)))
        for k in range(1, ngy)
    ]
    for c in tile_copies:
        c.start()
    disp_moves = [
        ((-1, 0), remote(drow, drow_in, s3.at[0], r3.at[0], (gx - 1, gy))),
        ((0, -1), remote(dcol, dcol_in.at[0:rows], s3.at[1], r3.at[1], (gx, gy - 1))),
        ((-1, -1), remote(dcol.at[0:8], dcol_in.at[rows : rows + 8], s3.at[2], r3.at[2], (gx - 1, gy - 1))),
    ]
    for (dx, dy), c in disp_moves:
        @pl.when(exists(dx, dy))
        def _(c=c):
            c.start()

    @pl.when(jnp.logical_not(down))
    def _():
        drow_in[...] = jnp.zeros(drow_in.shape, f32)

    @pl.when(jnp.logical_not(right))
    def _():
        dcol_in[0:rows] = jnp.zeros((rows, TILE), f32)

    @pl.when(jnp.logical_not(exists(1, 1)))
    def _():
        dcol_in[rows : rows + 8] = jnp.zeros((8, TILE), f32)

    def row_span(dx):
        return {1: slice(0, 8), 0: slice(8, 8 + rows), -1: slice(8 + rows, full)}[dx]

    def col_span(dx):
        return {1: slice(rows - 8, rows), 0: slice(0, rows), -1: slice(0, 8)}[dx]

    def halo_copy(n, dx, dy):
        to = (gx + dx, gy + dy)
        if dy == 0:
            src, dst = xs.at[1 if dx > 0 else 0], rows_in.at[0 if dx > 0 else 1]
        else:
            src = pk.at[col_span(dx)]
            dst = cols_in.at[0 if dy > 0 else 1, row_span(dx)]
        return remote(src, dst, s2.at[n], r2.at[n], to)

    directions = [(0, 1), (0, -1)] + diagonals + [(1, 0), (-1, 0)]
    halo = [(dx, dy, halo_copy(n, dx, dy)) for n, (dx, dy) in enumerate(directions)]
    for dx, dy, _c in halo:
        @pl.when(jnp.logical_not(exists(-dx, -dy)))
        def _(dx=dx, dy=dy):
            if dy == 0:
                rows_in[0 if dx > 0 else 1] = jnp.zeros(rows_in.shape[1:], f32)
            else:
                span = row_span(dx)
                cols_in[0 if dy > 0 else 1, span] = jnp.zeros((span.stop - span.start, TILE), f32)

    zero8 = jnp.zeros((8, ext), f32)
    for f in range(F):
        q[f, 0:8] = zero8
        q[f, full - 8 : full] = zero8

    for c in loads[4:]:
        c.wait()
    eye = iota((rows, rows), 0) == iota((rows, rows), 1)
    spread = jnp.concatenate(
        [jnp.where(eye, mat[c : c + 1, :].astype(f32), 0.0).astype(bf16) for c in range(per_row)], axis=0
    )
    primary[...] = jnp.dot(spread, jnp.ones((rows, TILE), bf16), preferred_element_type=f32)

    for c in tile_copies:
        c.wait_recv()
    label = got1[0, cap : cap + 8, 0:count]
    for k in range(1, ngy):
        label = label + got1[k, cap : cap + 8, 0:count]
    tiles = per_row * rows
    place = iota((tiles, count), 0)
    place = (place % rows) * per_row + place // rows + 1
    hit = (jnp.broadcast_to(label[0:1, :].astype(jnp.int32), (tiles, count)) == place).astype(f32)
    arrived = jnp.concatenate([got1[k, 0:cap, 0 : 3 * TILE] for k in range(ngy)], axis=0)
    mixed = pick(hit, arrived)
    second = jnp.dot(
        (hit * label[1:2, :]).astype(bf16), jnp.ones((count, TILE), bf16), preferred_element_type=f32
    )
    edge = []
    for c in [0] + list(range(per_row - 1, 0, -1)):
        at = slice(c * rows, (c + 1) * rows)
        lanes = slice(c * TILE, (c + 1) * TILE)
        fr, d2, e2 = (mixed[at, n * TILE : (n + 1) * TILE] for n in range(3))
        other_m = second[at]
        own_m = primary[at]
        d1 = density[:, lanes]
        e1 = energy[:, lanes]
        de1 = d1 * e1
        de2 = d2 * e2
        clear = 1.0 - fr
        for m in range(M):
            own = jnp.where(own_m == float(m), clear, 0.0)
            oth = jnp.where(other_m == m + 1.0, fr, 0.0)
            for n, value in enumerate((own + oth, own * d1 + oth * d2, own * de1 + oth * de2)):
                q[3 * m + n, 8 : 8 + rows, lanes] = value
    acc = jnp.zeros((rows, TILE), f32)
    for f in range(F):
        both = jnp.where(
            lane_r < TILE // 2, q[f, 8 : 8 + rows, 0:TILE], q[f, 8 : 8 + rows, width - TILE : width]
        )
        acc = jnp.where(lane_r // 4 == f, pltpu.roll(both, 4 * f + 2, 1), acc)
    pk[...] = acc
    for dx, dy, c in halo[:6]:
        @pl.when(exists(dx, dy))
        def _(c=c):
            c.start()
    for f in range(F):
        xs[0, 2 * f : 2 * f + 2] = q[f, 8:16, 0:width][0:2]
        xs[1, 2 * f : 2 * f + 2] = q[f, rows : rows + 8, 0:width][6:8]
    for dx, dy, c in halo[6:]:
        @pl.when(exists(dx, dy))
        def _(c=c):
            c.start()

    for (dx, dy), c in disp_moves:
        @pl.when(exists(-dx, -dy))
        def _(c=c):
            c.wait_recv()
    dc = dcol_in[...]
    for c in range(2):
        de[c, 0:rows, 0:width] = disp[c]
        de[c, rows : rows + 8, 0:width] = jnp.broadcast_to(drow_in[c : c + 1, :], (8, width))
        de[c, :, width:ext] = dc if c == 0 else pltpu.roll(dc, TILE - 1, 1)
    face = iota((rows + 8, ext), 0)
    closed_x = jnp.logical_or(
        jnp.logical_and(face == 0, jnp.logical_not(up)), jnp.logical_and(face == rows, jnp.logical_not(down))
    )
    d0 = de[0]
    speed = jnp.where(closed_x, 0.0, -0.5 * (d0 + pltpu.roll(d0, ext - 1, 1)))
    ax[...] = jnp.maximum(speed, 0.0)
    bx[...] = jnp.minimum(speed, 0.0)
    face = iota((rows, ext), 1)
    closed_y = jnp.logical_or(
        jnp.logical_and(face == 0, jnp.logical_not(left)), jnp.logical_and(face == width, jnp.logical_not(right))
    )
    d1 = de[1]
    speed = jnp.where(closed_y, 0.0, -0.5 * (d1[0:rows] + pltpu.roll(d1, rows + 7, 0)[0:rows]))
    ay[...] = jnp.maximum(speed, 0.0)
    by[...] = jnp.minimum(speed, 0.0)

    for dx, dy, c in halo:
        @pl.when(exists(-dx, -dy))
        def _(c=c):
            c.wait_recv()
    lane_f = iota((full, TILE), 1)
    ring = jnp.where(lane_f % 4 < 2, cols_in[0], cols_in[1])
    for f in range(F):
        q[f, :, width:ext] = pltpu.roll(ring, TILE - 4 * f - 2, 1)
        q[f, 6:8, 0:width] = rows_in[0, 2 * f : 2 * f + 2]
        q[f, 8 + rows : 10 + rows, 0:width] = rows_in[1, 2 * f : 2 * f + 2]

    blocks = full // 8
    sub = iota((8, ext), 0)
    twelfth = 1.0 / 12.0

    def one_field(f, carry):
        qs, sums, diffs, hs, fluxes = {}, {}, {}, {}, {}

        def load(b):
            if b not in qs:
                v = q[f, b * 8 : b * 8 + 8]
                before, after = pltpu.roll(v, 1, 1), pltpu.roll(v, ext - 1, 1)
                qs[b], sums[b], diffs[b] = v, v + before + after, after - before

        def prev(values, b):
            if b == 0:
                return pltpu.roll(values[b], 1, 0)
            return pltpu.roll(jnp.where(sub == 7, values[b - 1], values[b]), 1, 0)

        def follow(values, b):
            if b == blocks - 1:
                return pltpu.roll(values[b], 7, 0)
            return pltpu.roll(jnp.where(sub == 0, values[b + 1], values[b]), 7, 0)

        low, high = {}, {}

        def sides(b):
            if b not in low:
                for n in (b - 1, b, b + 1):
                    if 0 <= n < blocks:
                        load(n)
                h = (follow(sums, b) - prev(sums, b)) * twelfth
                low[b], high[b] = qs[b] + h, qs[b] - h

        def flux(b):
            if b not in fluxes:
                sides(b - 1)
                sides(b)
                at = slice(b * 8 - 8, b * 8)
                fluxes[b] = ax[at] * prev(low, b) + bx[at] * high[b]

        total = jnp.zeros((8, width), f32)
        for b in range(1, blocks - 1):
            flux(b)
            flux(b + 1)
            at = slice(b * 8 - 8, b * 8)
            h = (diffs[b] + prev(diffs, b) + follow(diffs, b)) * twelfth
            fy = ay[at] * pltpu.roll(qs[b] + h, 1, 1) + by[at] * (qs[b] - h)
            value = qs[b] + fluxes[b] - follow(fluxes, b) + fy - pltpu.roll(fy, ext - 1, 1)
            value = value[:, 0:width]
            out[f, at] = value
            total = total + value
        lanes = total[:, 0:TILE]
        for c in range(1, per_row):
            lanes = lanes + total[:, c * TILE : (c + 1) * TILE]
        part[f] = lanes
        pltpu.make_async_copy(out.at[f], out_h.at[f], so.at[f]).start()
        return carry

    lax.fori_loop(0, F, one_field, 0)

    mine = jnp.concatenate(
        [jnp.sum(part[3 * m + n], axis=0, keepdims=True) for m in range(M) for n in (1, 2)], axis=0
    )
    tot_y[gy] = mine
    copies = [
        remote(tot_y.at[gy], tot_y.at[gy], sy.at[k], ry.at[k], (gx, lax.rem(gy + k, ngy)))
        for k in range(1, ngy)
    ]
    for c in copies:
        c.start()
    incoming = [
        remote(tot_y.at[lax.rem(gy + ngy - k, ngy)], tot_y.at[lax.rem(gy + ngy - k, ngy)], sy.at[k], ry.at[k],
               (gx, lax.rem(gy + k, ngy)))
        for k in range(1, ngy)
    ]
    for c in incoming:
        c.wait_recv()
    mine = tot_y[0]
    for k in range(1, ngy):
        mine = mine + tot_y[k]
    tot_x[gx] = mine
    copies_x = [
        remote(tot_x.at[gx], tot_x.at[gx], sx.at[k], rx.at[k], (lax.rem(gx + k, ngx), gy))
        for k in range(1, ngx)
    ]
    for c in copies_x:
        c.start()
    incoming = [
        remote(tot_x.at[lax.rem(gx + ngx - k, ngx)], tot_x.at[lax.rem(gx + ngx - k, ngx)], sx.at[k], rx.at[k],
               (lax.rem(gx + k, ngx), gy))
        for k in range(1, ngx)
    ]
    for c in incoming:
        c.wait_recv()
    mine = tot_x[0]
    for k in range(1, ngx):
        mine = mine + tot_x[k]
    whole = jnp.broadcast_to(jnp.sum(mine, axis=1, keepdims=True), (2 * M, TILE))
    r8, l8 = iota((2 * M, TILE), 0), iota((2 * M, TILE), 1)
    for n in range(2):
        line = jnp.sum(jnp.where(r8 == 2 * l8 + n, whole, 0.0), axis=0, keepdims=True)
        totals[n : n + 1, :] = line[:, 0:M]

    for f in range(F):
        pltpu.make_async_copy(out.at[f], out_h.at[f], so.at[f]).wait()
    for c in tile_copies + copies + copies_x:
        c.wait_send()
    for (dx, dy), c in disp_moves:
        @pl.when(exists(dx, dy))
        def _(c=c):
            c.wait_send()
    for dx, dy, c in halo:
        @pl.when(exists(dx, dy))
        def _(c=c):
            c.wait_send()


def local(ngx, ngy, density, energy, displacement, tile_mat, store_frac, store_state, store_route):
    rows, width = density.shape
    cap = rows * (width // TILE) // 16
    ext, full = width + TILE, rows + 16
    wide = -(-max(3 * TILE, ngy * cap) // TILE) * TILE
    vmem, dma = pltpu.VMEM, pltpu.SemaphoreType.DMA
    spec = pl.BlockSpec(memory_space=pltpu.VMEM)
    far = pl.BlockSpec(memory_space=pltpu.HBM)
    inputs = (density, energy, displacement, tile_mat.T, store_frac, store_state, store_route)
    scratch = [
        vmem((F, rows, width), f32),
        dma((F,)),
        *(vmem(x.shape, x.dtype) for x in inputs),
        dma((7,)),
        vmem((rows * (width // TILE), TILE), f32),
        vmem((ngy, cap + 8, wide), f32),
        vmem((ngy, cap + 8, wide), f32),
        vmem((8, width), f32),
        vmem((8, width), f32),
        vmem((rows, TILE), f32),
        vmem((rows + 8, TILE), f32),
        vmem((2, rows + 8, ext), f32),
        vmem((rows + 8, ext), f32),
        vmem((rows + 8, ext), f32),
        vmem((rows, ext), f32),
        vmem((rows, ext), f32),
        vmem((F, full, ext), f32),
        vmem((rows, TILE), f32),
        vmem((2, 2 * F, width), f32),
        vmem((2, full, TILE), f32),
        vmem((2, 2 * F, width), f32),
        vmem((F, 8, TILE), f32),
        vmem((ngy, 2 * M, TILE), f32),
        vmem((ngx, 2 * M, TILE), f32),
        vmem((8, TILE), f32),
        dma((ngy,)), dma((ngy,)), dma((8,)), dma((8,)), dma((3,)), dma((3,)),
        dma((ngy,)), dma((ngy,)), dma((ngx,)), dma((ngx,)),
    ]
    remapped, totals = pl.pallas_call(
        functools.partial(kernel, ngx, ngy, cap),
        out_shape=(jax.ShapeDtypeStruct((F, rows, width), f32), jax.ShapeDtypeStruct((2, M), f32)),
        in_specs=[far] * 7,
        out_specs=(far, spec),
        scratch_shapes=scratch,
        compiler_params=pltpu.CompilerParams(
            collective_id=0, has_side_effects=True, vmem_limit_bytes=63 * 1024 * 1024
        ),
    )(*inputs)
    return remapped.reshape(M, 3, rows, width), totals


def solution(mesh):
    placed = (
        P("gx", "gy"),
        P("gx", "gy"),
        P(None, "gx", "gy"),
        P("gx", "gy"),
        P(("gx", "gy"), None),
        P(None, ("gx", "gy"), None),
        P(None, ("gx", "gy")),
    )
    return jax.shard_map(
        functools.partial(local, mesh.shape["gx"], mesh.shape["gy"]),
        mesh=mesh,
        in_specs=placed,
        out_specs=(P(None, None, "gx", "gy"), P()),
        check_vma=False,
    )
```

```python
import functools
import jax
import jax.numpy as jnp
from jax import lax
from jax.experimental import pallas as pl
from jax.experimental.pallas import tpu as pltpu
from jax.sharding import PartitionSpec as P

M = 4
F = 3 * M
TILE = 128
MESH = pl.DeviceIdType.MESH
f32 = jnp.float32
bf16 = jnp.bfloat16
NT = (((1,), (1,)), ((), ()))


def iota(shape, dim):
    return lax.broadcasted_iota(jnp.int32, shape, dim)


def split3(x):
    hi = x.astype(bf16)
    rest = x - hi.astype(f32)
    mid = rest.astype(bf16)
    low = (rest - mid.astype(f32)).astype(bf16)
    return hi, mid, low


def pick(onehot, data):
    parts = split3(data)
    o = onehot.astype(bf16)
    total = jnp.dot(o, parts[2], preferred_element_type=f32)
    total = total + jnp.dot(o, parts[1], preferred_element_type=f32)
    return total + jnp.dot(o, parts[0], preferred_element_type=f32)


def kernel(
    ngx, ngy, cap,
    density_h, energy_h, disp_h, mat_h, frac_h, state_h, route_h,
    out, totals,
    density, energy, disp, mat, frac, state, route, s0,
    primary, send1, got1, drow, drow_in, dcol, dcol_in, de, ax, bx, ay, by,
    q, pk, xs, cols_in, rows_in, part, tot_y, tot_x, tot_sum,
    s1, r1, s2, r2, s3, r3, sy, ry, sx, rx,
):
    gx, gy = lax.axis_index("gx"), lax.axis_index("gy")
    rows, width = density.shape
    ext = width + TILE
    full = rows + 16
    per_row = width // TILE
    slots = frac.shape[0]
    up, down = gx > 0, gx < ngx - 1
    left, right = gy > 0, gy < ngy - 1

    def exists(dx, dy):
        ok = True
        if dx:
            ok = up if dx < 0 else down
        if dy:
            side = left if dy < 0 else right
            ok = side if ok is True else jnp.logical_and(ok, side)
        return ok

    loads = [
        pltpu.make_async_copy(src, dst, s0.at[n])
        for n, (src, dst) in enumerate(
            (
                (route_h, route), (frac_h, frac), (state_h, state), (disp_h, disp),
                (mat_h, mat), (density_h, density), (energy_h, energy),
            )
        )
    ]
    for c in loads:
        c.start()

    barrier = pltpu.get_barrier_semaphore()
    diagonals = [(-1, -1), (-1, 1), (1, -1), (1, 1)]
    for k in range(1, ngy):
        pl.semaphore_signal(barrier, inc=1, device_id=(gx, lax.rem(gy + k, ngy)), device_id_type=MESH)
    for k in range(1, ngx):
        pl.semaphore_signal(barrier, inc=1, device_id=(lax.rem(gx + k, ngx), gy), device_id_type=MESH)
    for dx, dy in diagonals:
        @pl.when(exists(dx, dy))
        def _(dx=dx, dy=dy):
            pl.semaphore_signal(barrier, inc=1, device_id=(gx + dx, gy + dy), device_id_type=MESH)

    count = ngy * cap
    loads[0].wait()
    target = route[0:1, :]
    row = iota((count, slots), 0)
    wanted = lax.rem(gy + row // cap, ngy)
    member = (jnp.broadcast_to(target, (count, slots)) == wanted).astype(f32)
    before = (iota((slots, slots), 0) < iota((slots, slots), 1)).astype(bf16)
    rank = jnp.dot(member.astype(bf16), before, preferred_element_type=f32)
    chosen = jnp.where(rank == (row % cap).astype(f32), member, 0.0)
    loads[1].wait()
    loads[2].wait()
    payload = jnp.concatenate([frac[...], state[0], state[1]], axis=1)
    packed = pick(chosen, payload)
    named = jnp.concatenate(
        [(route[1:3, :] + 1).astype(f32), jnp.zeros((6, slots), f32)], axis=0
    )
    labels = lax.dot_general(
        named, chosen, NT, precision=lax.Precision.HIGHEST, preferred_element_type=f32
    )
    label_lane = iota((8, count), 1) // cap
    wide = send1.shape[2]
    for k in range(ngy):
        dst = got1 if k == 0 else send1
        dst[k, 0:cap, 0 : 3 * TILE] = packed[k * cap : (k + 1) * cap]
        dst[k, cap : cap + 8, 0:count] = jnp.where(label_lane == k, labels, 0.0)

    loads[3].wait()
    drow[...] = jnp.concatenate([disp[0, 0:8][0:1], disp[1, 0:8][0:1], jnp.zeros((6, width), f32)], axis=0)
    lane_r = iota((rows, TILE), 1)
    dcol[...] = jnp.where(lane_r == 0, disp[0, :, 0:TILE], pltpu.roll(disp[1, :, 0:TILE], 1, 1))

    diag_count = sum(exists(dx, dy).astype(jnp.int32) for dx, dy in diagonals)
    pl.semaphore_wait(barrier, ngy - 1 + ngx - 1 + diag_count)

    def remote(src, dst, s, r, to):
        return pltpu.make_async_remote_copy(
            src_ref=src, dst_ref=dst, send_sem=s, recv_sem=r, device_id=to, device_id_type=MESH
        )

    tile_copies = [
        remote(send1.at[k], got1.at[k], s1.at[k], r1.at[k], (gx, lax.rem(gy + k, ngy)))
        for k in range(1, ngy)
    ]
    for c in tile_copies:
        c.start()
    disp_moves = [
        ((-1, 0), remote(drow, drow_in, s3.at[0], r3.at[0], (gx - 1, gy))),
        ((0, -1), remote(dcol, dcol_in.at[0:rows], s3.at[1], r3.at[1], (gx, gy - 1))),
        ((-1, -1), remote(dcol.at[0:8], dcol_in.at[rows : rows + 8], s3.at[2], r3.at[2], (gx - 1, gy - 1))),
    ]
    for (dx, dy), c in disp_moves:
        @pl.when(exists(dx, dy))
        def _(c=c):
            c.start()

    @pl.when(jnp.logical_not(down))
    def _():
        drow_in[...] = jnp.zeros(drow_in.shape, f32)

    @pl.when(jnp.logical_not(right))
    def _():
        dcol_in[0:rows] = jnp.zeros((rows, TILE), f32)

    @pl.when(jnp.logical_not(exists(1, 1)))
    def _():
        dcol_in[rows : rows + 8] = jnp.zeros((8, TILE), f32)

    def row_span(dx):
        return {1: slice(0, 8), 0: slice(8, 8 + rows), -1: slice(8 + rows, full)}[dx]

    def col_span(dx):
        return {1: slice(rows - 8, rows), 0: slice(0, rows), -1: slice(0, 8)}[dx]

    def halo_copy(n, dx, dy):
        to = (gx + dx, gy + dy)
        if dy == 0:
            src, dst = xs.at[1 if dx > 0 else 0], rows_in.at[0 if dx > 0 else 1]
        else:
            src = pk.at[col_span(dx)]
            dst = cols_in.at[0 if dy > 0 else 1, row_span(dx)]
        return remote(src, dst, s2.at[n], r2.at[n], to)

    directions = [(0, 1), (0, -1)] + diagonals + [(1, 0), (-1, 0)]
    halo = [(dx, dy, halo_copy(n, dx, dy)) for n, (dx, dy) in enumerate(directions)]
    for dx, dy, _c in halo:
        @pl.when(jnp.logical_not(exists(-dx, -dy)))
        def _(dx=dx, dy=dy):
            if dy == 0:
                rows_in[0 if dx > 0 else 1] = jnp.zeros(rows_in.shape[1:], f32)
            else:
                span = row_span(dx)
                cols_in[0 if dy > 0 else 1, span] = jnp.zeros((span.stop - span.start, TILE), f32)

    zero8 = jnp.zeros((8, ext), f32)
    for f in range(F):
        q[f, 0:8] = zero8
        q[f, full - 8 : full] = zero8

    for c in loads[4:]:
        c.wait()
    eye = iota((rows, rows), 0) == iota((rows, rows), 1)
    spread = jnp.concatenate(
        [jnp.where(eye, mat[c : c + 1, :].astype(f32), 0.0).astype(bf16) for c in range(per_row)], axis=0
    )
    primary[...] = jnp.dot(spread, jnp.ones((rows, TILE), bf16), preferred_element_type=f32)

    for c in tile_copies:
        c.wait_recv()
    label = got1[0, cap : cap + 8, 0:count]
    for k in range(1, ngy):
        label = label + got1[k, cap : cap + 8, 0:count]
    tiles = per_row * rows
    place = iota((tiles, count), 0)
    place = (place % rows) * per_row + place // rows + 1
    hit = (jnp.broadcast_to(label[0:1, :].astype(jnp.int32), (tiles, count)) == place).astype(f32)
    arrived = jnp.concatenate([got1[k, 0:cap, 0 : 3 * TILE] for k in range(ngy)], axis=0)
    mixed = pick(hit, arrived)
    second = jnp.dot(
        (hit * label[1:2, :]).astype(bf16), jnp.ones((count, TILE), bf16), preferred_element_type=f32
    )
    edge = []
    for c in [0] + list(range(per_row - 1, 0, -1)):
        at = slice(c * rows, (c + 1) * rows)
        lanes = slice(c * TILE, (c + 1) * TILE)
        fr, d2, e2 = (mixed[at, n * TILE : (n + 1) * TILE] for n in range(3))
        other_m = second[at]
        own_m = primary[at]
        d1 = density[:, lanes]
        e1 = energy[:, lanes]
        de1 = d1 * e1
        de2 = d2 * e2
        clear = 1.0 - fr
        for m in range(M):
            own = jnp.where(own_m == float(m), clear, 0.0)
            oth = jnp.where(other_m == m + 1.0, fr, 0.0)
            for n, value in enumerate((own + oth, own * d1 + oth * d2, own * de1 + oth * de2)):
                q[3 * m + n, 8 : 8 + rows, lanes] = value
    acc = jnp.zeros((rows, TILE), f32)
    for f in range(F):
        both = jnp.where(
            lane_r < TILE // 2, q[f, 8 : 8 + rows, 0:TILE], q[f, 8 : 8 + rows, width - TILE : width]
        )
        acc = jnp.where(lane_r // 4 == f, pltpu.roll(both, 4 * f + 2, 1), acc)
    pk[...] = acc
    for dx, dy, c in halo[:6]:
        @pl.when(exists(dx, dy))
        def _(c=c):
            c.start()
    for f in range(F):
        xs[0, 2 * f : 2 * f + 2] = q[f, 8:16, 0:width][0:2]
        xs[1, 2 * f : 2 * f + 2] = q[f, rows : rows + 8, 0:width][6:8]
    for dx, dy, c in halo[6:]:
        @pl.when(exists(dx, dy))
        def _(c=c):
            c.start()

    for (dx, dy), c in disp_moves:
        @pl.when(exists(-dx, -dy))
        def _(c=c):
            c.wait_recv()
    dc = dcol_in[...]
    for c in range(2):
        de[c, 0:rows, 0:width] = disp[c]
        de[c, rows : rows + 8, 0:width] = jnp.broadcast_to(drow_in[c : c + 1, :], (8, width))
        de[c, :, width:ext] = dc if c == 0 else pltpu.roll(dc, TILE - 1, 1)
    face = iota((rows + 8, ext), 0)
    closed_x = jnp.logical_or(
        jnp.logical_and(face == 0, jnp.logical_not(up)), jnp.logical_and(face == rows, jnp.logical_not(down))
    )
    d0 = de[0]
    speed = jnp.where(closed_x, 0.0, -0.5 * (d0 + pltpu.roll(d0, ext - 1, 1)))
    ax[...] = jnp.maximum(speed, 0.0)
    bx[...] = jnp.minimum(speed, 0.0)
    face = iota((rows, ext), 1)
    closed_y = jnp.logical_or(
        jnp.logical_and(face == 0, jnp.logical_not(left)), jnp.logical_and(face == width, jnp.logical_not(right))
    )
    d1 = de[1]
    speed = jnp.where(closed_y, 0.0, -0.5 * (d1[0:rows] + pltpu.roll(d1, rows + 7, 0)[0:rows]))
    ay[...] = jnp.maximum(speed, 0.0)
    by[...] = jnp.minimum(speed, 0.0)

    for dx, dy, c in halo:
        @pl.when(exists(-dx, -dy))
        def _(c=c):
            c.wait_recv()
    lane_f = iota((full, TILE), 1)
    ring = jnp.where(lane_f % 4 < 2, cols_in[0], cols_in[1])
    for f in range(F):
        q[f, :, width:ext] = pltpu.roll(ring, TILE - 4 * f - 2, 1)
        q[f, 6:8, 0:width] = rows_in[0, 2 * f : 2 * f + 2]
        q[f, 8 + rows : 10 + rows, 0:width] = rows_in[1, 2 * f : 2 * f + 2]

    blocks = full // 8
    sub = iota((8, ext), 0)
    twelfth = 1.0 / 12.0

    def one_field(f, carry):
        qs, sums, diffs, hs, fluxes = {}, {}, {}, {}, {}

        def load(b):
            if b not in qs:
                v = q[f, b * 8 : b * 8 + 8]
                before, after = pltpu.roll(v, 1, 1), pltpu.roll(v, ext - 1, 1)
                qs[b], sums[b], diffs[b] = v, v + before + after, after - before

        def prev(values, b):
            if b == 0:
                return pltpu.roll(values[b], 1, 0)
            return pltpu.roll(jnp.where(sub == 7, values[b - 1], values[b]), 1, 0)

        def follow(values, b):
            if b == blocks - 1:
                return pltpu.roll(values[b], 7, 0)
            return pltpu.roll(jnp.where(sub == 0, values[b + 1], values[b]), 7, 0)

        low, high = {}, {}

        def sides(b):
            if b not in low:
                for n in (b - 1, b, b + 1):
                    if 0 <= n < blocks:
                        load(n)
                h = (follow(sums, b) - prev(sums, b)) * twelfth
                low[b], high[b] = qs[b] + h, qs[b] - h

        def flux(b):
            if b not in fluxes:
                sides(b - 1)
                sides(b)
                at = slice(b * 8 - 8, b * 8)
                fluxes[b] = ax[at] * prev(low, b) + bx[at] * high[b]

        total = jnp.zeros((8, width), f32)
        for b in range(1, blocks - 1):
            flux(b)
            flux(b + 1)
            at = slice(b * 8 - 8, b * 8)
            h = (diffs[b] + prev(diffs, b) + follow(diffs, b)) * twelfth
            fy = ay[at] * pltpu.roll(qs[b] + h, 1, 1) + by[at] * (qs[b] - h)
            value = qs[b] + fluxes[b] - follow(fluxes, b) + fy - pltpu.roll(fy, ext - 1, 1)
            value = value[:, 0:width]
            out[f, at] = value
            total = total + value
        lanes = total[:, 0:TILE]
        for c in range(1, per_row):
            lanes = lanes + total[:, c * TILE : (c + 1) * TILE]
        part[f] = lanes
        return carry

    lax.fori_loop(0, F, one_field, 0)

    mine = jnp.concatenate(
        [jnp.sum(part[3 * m + n], axis=0, keepdims=True) for m in range(M) for n in (1, 2)], axis=0
    )
    tot_y[gy] = mine
    copies = [
        remote(tot_y.at[gy], tot_y.at[gy], sy.at[k], ry.at[k], (gx, lax.rem(gy + k, ngy)))
        for k in range(1, ngy)
    ]
    for c in copies:
        c.start()
    incoming = [
        remote(tot_y.at[lax.rem(gy + ngy - k, ngy)], tot_y.at[lax.rem(gy + ngy - k, ngy)], sy.at[k], ry.at[k],
               (gx, lax.rem(gy + k, ngy)))
        for k in range(1, ngy)
    ]
    for c in incoming:
        c.wait_recv()
    mine = tot_y[0]
    for k in range(1, ngy):
        mine = mine + tot_y[k]
    tot_x[gx] = mine
    copies_x = [
        remote(tot_x.at[gx], tot_x.at[gx], sx.at[k], rx.at[k], (lax.rem(gx + k, ngx), gy))
        for k in range(1, ngx)
    ]
    for c in copies_x:
        c.start()
    incoming = [
        remote(tot_x.at[lax.rem(gx + ngx - k, ngx)], tot_x.at[lax.rem(gx + ngx - k, ngx)], sx.at[k], rx.at[k],
               (lax.rem(gx + k, ngx), gy))
        for k in range(1, ngx)
    ]
    for c in incoming:
        c.wait_recv()
    mine = tot_x[0]
    for k in range(1, ngx):
        mine = mine + tot_x[k]
    whole = jnp.broadcast_to(jnp.sum(mine, axis=1, keepdims=True), (2 * M, TILE))
    r8, l8 = iota((2 * M, TILE), 0), iota((2 * M, TILE), 1)
    for n in range(2):
        line = jnp.sum(jnp.where(r8 == 2 * l8 + n, whole, 0.0), axis=0, keepdims=True)
        totals[n : n + 1, :] = line[:, 0:M]

    for c in tile_copies + copies + copies_x:
        c.wait_send()
    for (dx, dy), c in disp_moves:
        @pl.when(exists(dx, dy))
        def _(c=c):
            c.wait_send()
    for dx, dy, c in halo:
        @pl.when(exists(dx, dy))
        def _(c=c):
            c.wait_send()


def local(ngx, ngy, density, energy, displacement, tile_mat, store_frac, store_state, store_route):
    rows, width = density.shape
    cap = rows * (width // TILE) // 16
    ext, full = width + TILE, rows + 16
    wide = -(-max(3 * TILE, ngy * cap) // TILE) * TILE
    vmem, dma = pltpu.VMEM, pltpu.SemaphoreType.DMA
    spec = pl.BlockSpec(memory_space=pltpu.VMEM)
    far = pl.BlockSpec(memory_space=pltpu.HBM)
    inputs = (density, energy, displacement, tile_mat.T, store_frac, store_state, store_route)
    scratch = [
        *(vmem(x.shape, x.dtype) for x in inputs),
        dma((7,)),
        vmem((rows * (width // TILE), TILE), f32),
        vmem((ngy, cap + 8, wide), f32),
        vmem((ngy, cap + 8, wide), f32),
        vmem((8, width), f32),
        vmem((8, width), f32),
        vmem((rows, TILE), f32),
        vmem((rows + 8, TILE), f32),
        vmem((2, rows + 8, ext), f32),
        vmem((rows + 8, ext), f32),
        vmem((rows + 8, ext), f32),
        vmem((rows, ext), f32),
        vmem((rows, ext), f32),
        vmem((F, full, ext), f32),
        vmem((rows, TILE), f32),
        vmem((2, 2 * F, width), f32),
        vmem((2, full, TILE), f32),
        vmem((2, 2 * F, width), f32),
        vmem((F, 8, TILE), f32),
        vmem((ngy, 2 * M, TILE), f32),
        vmem((ngx, 2 * M, TILE), f32),
        vmem((8, TILE), f32),
        dma((ngy,)), dma((ngy,)), dma((8,)), dma((8,)), dma((3,)), dma((3,)),
        dma((ngy,)), dma((ngy,)), dma((ngx,)), dma((ngx,)),
    ]
    remapped, totals = pl.pallas_call(
        functools.partial(kernel, ngx, ngy, cap),
        out_shape=(pltpu.VMEM((F, rows, width), f32), jax.ShapeDtypeStruct((2, M), f32)),
        in_specs=[far] * 7,
        out_specs=(spec, spec),
        scratch_shapes=scratch,
        compiler_params=pltpu.CompilerParams(
            collective_id=0, has_side_effects=True, vmem_limit_bytes=61 * 1024 * 1024
        ),
    )(*inputs)
    return remapped.reshape(M, 3, rows, width), totals


def solution(mesh):
    placed = (
        P("gx", "gy"),
        P("gx", "gy"),
        P(None, "gx", "gy"),
        P("gx", "gy"),
        P(("gx", "gy"), None),
        P(None, ("gx", "gy"), None),
        P(None, ("gx", "gy")),
    )
    return jax.shard_map(
        functools.partial(local, mesh.shape["gx"], mesh.shape["gy"]),
        mesh=mesh,
        in_specs=placed,
        out_specs=(P(None, None, "gx", "gy"), P()),
        check_vma=False,
    )
```

```python
import functools
import jax
import jax.numpy as jnp
from jax import lax
from jax.experimental import pallas as pl
from jax.experimental.pallas import tpu as pltpu
from jax.sharding import PartitionSpec as P

M = 4
F = 3 * M
TILE = 128
MESH = pl.DeviceIdType.MESH
f32 = jnp.float32
bf16 = jnp.bfloat16
NT = (((1,), (1,)), ((), ()))


def iota(shape, dim):
    return lax.broadcasted_iota(jnp.int32, shape, dim)


def split2(x):
    hi = x.astype(bf16)
    rest = x - hi.astype(f32)
    return hi, rest.astype(bf16)


def pick(onehot, data):
    parts = split2(data)
    o = onehot.astype(bf16)
    low = jnp.dot(o, parts[1], preferred_element_type=f32)
    return low + jnp.dot(o, parts[0], preferred_element_type=f32)


def kernel(
    ngx, ngy, cap,
    density_h, energy_h, disp_h, mat_h, frac_h, state_h, route_h,
    out, totals,
    density, energy, disp, mat, frac, state, route, s0,
    primary, send1, got1, drow, drow_in, dcol, dcol_in, de, ax, bx, ay, by,
    q, pk, xs, cols_in, rows_in, part, tot_y, tot_x, tot_sum,
    s1, r1, s2, r2, s3, r3, sy, ry, sx, rx,
):
    gx, gy = lax.axis_index("gx"), lax.axis_index("gy")
    rows, width = density.shape
    ext = width + TILE
    full = rows + 16
    per_row = width // TILE
    slots = frac.shape[0]
    up, down = gx > 0, gx < ngx - 1
    left, right = gy > 0, gy < ngy - 1

    def exists(dx, dy):
        ok = True
        if dx:
            ok = up if dx < 0 else down
        if dy:
            side = left if dy < 0 else right
            ok = side if ok is True else jnp.logical_and(ok, side)
        return ok

    loads = [
        pltpu.make_async_copy(src, dst, s0.at[n])
        for n, (src, dst) in enumerate(
            (
                (route_h, route), (frac_h, frac), (state_h, state), (disp_h, disp),
                (mat_h, mat), (density_h, density), (energy_h, energy),
            )
        )
    ]
    for c in loads[:3]:
        c.start()

    barrier = pltpu.get_barrier_semaphore()
    diagonals = [(-1, -1), (-1, 1), (1, -1), (1, 1)]
    for k in range(1, ngy):
        pl.semaphore_signal(barrier, inc=1, device_id=(gx, lax.rem(gy + k, ngy)), device_id_type=MESH)
    for k in range(1, ngx):
        pl.semaphore_signal(barrier, inc=1, device_id=(lax.rem(gx + k, ngx), gy), device_id_type=MESH)
    for dx, dy in diagonals:
        @pl.when(exists(dx, dy))
        def _(dx=dx, dy=dy):
            pl.semaphore_signal(barrier, inc=1, device_id=(gx + dx, gy + dy), device_id_type=MESH)

    for c in loads[3:]:
        c.start()

    count = ngy * cap
    loads[0].wait()
    target = route[0:1, :]
    row = iota((count, slots), 0)
    wanted = lax.rem(gy + row // cap, ngy)
    member = (jnp.broadcast_to(target, (count, slots)) == wanted).astype(f32)
    before = (iota((slots, slots), 0) < iota((slots, slots), 1)).astype(bf16)
    rank = jnp.dot(member.astype(bf16), before, preferred_element_type=f32)
    chosen = jnp.where(rank == (row % cap).astype(f32), member, 0.0)
    loads[1].wait()
    loads[2].wait()
    payload = jnp.concatenate([frac[...], state[0], state[1]], axis=1)
    packed = pick(chosen, payload)
    named = jnp.concatenate(
        [
            ((route[1:2, :] + 1) // 128).astype(f32), (route[2:3, :] + 1).astype(f32),
            ((route[1:2, :] + 1) % 128).astype(f32), jnp.zeros((5, slots), f32),
        ],
        axis=0,
    )
    labels = lax.dot_general(named.astype(bf16), chosen.astype(bf16), NT, preferred_element_type=f32)
    label_lane = iota((8, count), 1) // cap
    wide = send1.shape[2]
    for k in range(ngy):
        dst = got1 if k == 0 else send1
        dst[k, 0:cap, 0 : 3 * TILE] = packed[k * cap : (k + 1) * cap]
        dst[k, cap : cap + 8, 0:count] = jnp.where(label_lane == k, labels, 0.0)

    loads[3].wait()
    drow[...] = jnp.concatenate([disp[0, 0:8][0:1], disp[1, 0:8][0:1], jnp.zeros((6, width), f32)], axis=0)
    lane_r = iota((rows, TILE), 1)
    dcol[...] = jnp.where(lane_r == 0, disp[0, :, 0:TILE], pltpu.roll(disp[1, :, 0:TILE], 1, 1))

    diag_count = sum(exists(dx, dy).astype(jnp.int32) for dx, dy in diagonals)
    pl.semaphore_wait(barrier, ngy - 1 + ngx - 1 + diag_count)

    def remote(src, dst, s, r, to):
        return pltpu.make_async_remote_copy(
            src_ref=src, dst_ref=dst, send_sem=s, recv_sem=r, device_id=to, device_id_type=MESH
        )

    tile_copies = [
        remote(send1.at[k], got1.at[k], s1.at[k], r1.at[k], (gx, lax.rem(gy + k, ngy)))
        for k in range(1, ngy)
    ]
    for c in tile_copies:
        c.start()
    disp_moves = [
        ((-1, 0), remote(drow, drow_in, s3.at[0], r3.at[0], (gx - 1, gy))),
        ((0, -1), remote(dcol, dcol_in.at[0:rows], s3.at[1], r3.at[1], (gx, gy - 1))),
        ((-1, -1), remote(dcol.at[0:8], dcol_in.at[rows : rows + 8], s3.at[2], r3.at[2], (gx - 1, gy - 1))),
    ]
    for (dx, dy), c in disp_moves:
        @pl.when(exists(dx, dy))
        def _(c=c):
            c.start()

    @pl.when(jnp.logical_not(down))
    def _():
        drow_in[...] = jnp.zeros(drow_in.shape, f32)

    @pl.when(jnp.logical_not(right))
    def _():
        dcol_in[0:rows] = jnp.zeros((rows, TILE), f32)

    @pl.when(jnp.logical_not(exists(1, 1)))
    def _():
        dcol_in[rows : rows + 8] = jnp.zeros((8, TILE), f32)

    def row_span(dx):
        return {1: slice(0, 8), 0: slice(8, 8 + rows), -1: slice(8 + rows, full)}[dx]

    def col_span(dx):
        return {1: slice(rows - 8, rows), 0: slice(0, rows), -1: slice(0, 8)}[dx]

    def halo_copy(n, dx, dy):
        to = (gx + dx, gy + dy)
        if dy == 0:
            src, dst = xs.at[1 if dx > 0 else 0], rows_in.at[0 if dx > 0 else 1]
        else:
            src = pk.at[col_span(dx)]
            dst = cols_in.at[0 if dy > 0 else 1, row_span(dx)]
        return remote(src, dst, s2.at[n], r2.at[n], to)

    directions = [(0, 1), (0, -1)] + diagonals + [(1, 0), (-1, 0)]
    halo = [(dx, dy, halo_copy(n, dx, dy)) for n, (dx, dy) in enumerate(directions)]
    for dx, dy, _c in halo:
        @pl.when(jnp.logical_not(exists(-dx, -dy)))
        def _(dx=dx, dy=dy):
            if dy == 0:
                rows_in[0 if dx > 0 else 1] = jnp.zeros(rows_in.shape[1:], f32)
            else:
                span = row_span(dx)
                cols_in[0 if dy > 0 else 1, span] = jnp.zeros((span.stop - span.start, TILE), f32)

    zero8 = jnp.zeros((8, ext), f32)
    for f in range(F):
        q[f, 0:8] = zero8
        q[f, full - 8 : full] = zero8

    for c in loads[4:]:
        c.wait()
    eye = iota((rows, rows), 0) == iota((rows, rows), 1)
    spread = jnp.concatenate(
        [jnp.where(eye, mat[c : c + 1, :].astype(f32), 0.0).astype(bf16) for c in range(per_row)], axis=0
    )
    primary[...] = jnp.dot(spread, jnp.ones((rows, TILE), bf16), preferred_element_type=f32)

    for c in tile_copies:
        c.wait_recv()
    label = got1[0, cap : cap + 8, 0:count]
    for k in range(1, ngy):
        label = label + got1[k, cap : cap + 8, 0:count]
    tiles = per_row * rows
    place = iota((tiles, count), 0)
    place = (place % rows) * per_row + place // rows + 1
    tile_at = (label[0:1, :] * 128.0 + label[2:3, :]).astype(jnp.int32)
    hit = (jnp.broadcast_to(tile_at, (tiles, count)) == place).astype(f32)
    arrived = jnp.concatenate([got1[k, 0:cap, 0 : 3 * TILE] for k in range(ngy)], axis=0)
    mixed = pick(hit, arrived)
    second = jnp.dot(
        (hit * label[1:2, :]).astype(bf16), jnp.ones((count, TILE), bf16), preferred_element_type=f32
    )
    edge = []
    for c in [0] + list(range(per_row - 1, 0, -1)):
        at = slice(c * rows, (c + 1) * rows)
        lanes = slice(c * TILE, (c + 1) * TILE)
        fr, d2, e2 = (mixed[at, n * TILE : (n + 1) * TILE] for n in range(3))
        other_m = second[at]
        own_m = primary[at]
        d1 = density[:, lanes]
        e1 = energy[:, lanes]
        de1 = d1 * e1
        de2 = d2 * e2
        clear = 1.0 - fr
        for m in range(M):
            own = jnp.where(own_m == float(m), clear, 0.0)
            oth = jnp.where(other_m == m + 1.0, fr, 0.0)
            for n, value in enumerate((own + oth, own * d1 + oth * d2, own * de1 + oth * de2)):
                q[3 * m + n, 8 : 8 + rows, lanes] = value
    for f in range(F):
        xs[0, 2 * f : 2 * f + 2] = q[f, 8:16, 0:width][0:2]
        xs[1, 2 * f : 2 * f + 2] = q[f, rows : rows + 8, 0:width][6:8]
    for dx, dy, c in halo[6:]:
        @pl.when(exists(dx, dy))
        def _(c=c):
            c.start()
    acc = jnp.zeros((rows, TILE), f32)
    for f in range(F):
        both = jnp.where(
            lane_r < TILE // 2, q[f, 8 : 8 + rows, 0:TILE], q[f, 8 : 8 + rows, width - TILE : width]
        )
        acc = jnp.where(lane_r // 4 == f, pltpu.roll(both, 4 * f + 2, 1), acc)
    pk[...] = acc
    for dx, dy, c in halo[:6]:
        @pl.when(exists(dx, dy))
        def _(c=c):
            c.start()

    for (dx, dy), c in disp_moves:
        @pl.when(exists(-dx, -dy))
        def _(c=c):
            c.wait_recv()
    dc = dcol_in[...]
    for c in range(2):
        de[c, 0:rows, 0:width] = disp[c]
        de[c, rows : rows + 8, 0:width] = jnp.broadcast_to(drow_in[c : c + 1, :], (8, width))
        de[c, :, width:ext] = dc if c == 0 else pltpu.roll(dc, TILE - 1, 1)
    face = iota((rows + 8, ext), 0)
    closed_x = jnp.logical_or(
        jnp.logical_and(face == 0, jnp.logical_not(up)), jnp.logical_and(face == rows, jnp.logical_not(down))
    )
    d0 = de[0]
    speed = jnp.where(closed_x, 0.0, -0.5 * (d0 + pltpu.roll(d0, ext - 1, 1)))
    ax[...] = jnp.maximum(speed, 0.0)
    bx[...] = jnp.minimum(speed, 0.0)
    face = iota((rows, ext), 1)
    closed_y = jnp.logical_or(
        jnp.logical_and(face == 0, jnp.logical_not(left)), jnp.logical_and(face == width, jnp.logical_not(right))
    )
    d1 = de[1]
    speed = jnp.where(closed_y, 0.0, -0.5 * (d1[0:rows] + pltpu.roll(d1, rows + 7, 0)[0:rows]))
    ay[...] = jnp.maximum(speed, 0.0)
    by[...] = jnp.minimum(speed, 0.0)

    for dx, dy, c in halo:
        @pl.when(exists(-dx, -dy))
        def _(c=c):
            c.wait_recv()
    lane_f = iota((full, TILE), 1)
    ring = jnp.where(lane_f % 4 < 2, cols_in[0], cols_in[1])
    for f in range(F):
        q[f, :, width:ext] = pltpu.roll(ring, TILE - 4 * f - 2, 1)
        q[f, 6:8, 0:width] = rows_in[0, 2 * f : 2 * f + 2]
        q[f, 8 + rows : 10 + rows, 0:width] = rows_in[1, 2 * f : 2 * f + 2]

    blocks = full // 8
    sub = iota((8, ext), 0)
    twelfth = 1.0 / 12.0

    def one_field(f, carry):
        qs, sums, diffs, hs, fluxes = {}, {}, {}, {}, {}

        def load(b):
            if b not in qs:
                v = q[f, b * 8 : b * 8 + 8]
                before, after = pltpu.roll(v, 1, 1), pltpu.roll(v, ext - 1, 1)
                qs[b], sums[b], diffs[b] = v, v + before + after, after - before

        def prev(values, b):
            if b == 0:
                return pltpu.roll(values[b], 1, 0)
            return pltpu.roll(jnp.where(sub == 7, values[b - 1], values[b]), 1, 0)

        def follow(values, b):
            if b == blocks - 1:
                return pltpu.roll(values[b], 7, 0)
            return pltpu.roll(jnp.where(sub == 0, values[b + 1], values[b]), 7, 0)

        low, high = {}, {}

        def sides(b):
            if b not in low:
                for n in (b - 1, b, b + 1):
                    if 0 <= n < blocks:
                        load(n)
                h = (follow(sums, b) - prev(sums, b)) * twelfth
                low[b], high[b] = qs[b] + h, qs[b] - h

        def flux(b):
            if b not in fluxes:
                sides(b - 1)
                sides(b)
                at = slice(b * 8 - 8, b * 8)
                fluxes[b] = ax[at] * prev(low, b) + bx[at] * high[b]

        total = jnp.zeros((8, width), f32)
        for b in range(1, blocks - 1):
            flux(b)
            flux(b + 1)
            at = slice(b * 8 - 8, b * 8)
            h = (diffs[b] + prev(diffs, b) + follow(diffs, b)) * twelfth
            fy = ay[at] * pltpu.roll(qs[b] + h, 1, 1) + by[at] * (qs[b] - h)
            value = qs[b] + fluxes[b] - follow(fluxes, b) + fy - pltpu.roll(fy, ext - 1, 1)
            value = value[:, 0:width]
            out[f, at] = value
            total = total + value
        lanes = total[:, 0:TILE]
        for c in range(1, per_row):
            lanes = lanes + total[:, c * TILE : (c + 1) * TILE]
        part[f] = lanes
        return carry

    lax.fori_loop(0, F, one_field, 0)

    mine = jnp.concatenate(
        [jnp.sum(part[3 * m + n], axis=0, keepdims=True) for m in range(M) for n in (1, 2)], axis=0
    )
    tot_y[gy] = mine
    copies = [
        remote(tot_y.at[gy], tot_y.at[gy], sy.at[k], ry.at[k], (gx, lax.rem(gy + k, ngy)))
        for k in range(1, ngy)
    ]
    for c in copies:
        c.start()
    incoming = [
        remote(tot_y.at[lax.rem(gy + ngy - k, ngy)], tot_y.at[lax.rem(gy + ngy - k, ngy)], sy.at[k], ry.at[k],
               (gx, lax.rem(gy + k, ngy)))
        for k in range(1, ngy)
    ]
    for c in incoming:
        c.wait_recv()
    mine = tot_y[0]
    for k in range(1, ngy):
        mine = mine + tot_y[k]
    tot_x[gx] = mine
    copies_x = [
        remote(tot_x.at[gx], tot_x.at[gx], sx.at[k], rx.at[k], (lax.rem(gx + k, ngx), gy))
        for k in range(1, ngx)
    ]
    for c in copies_x:
        c.start()
    incoming = [
        remote(tot_x.at[lax.rem(gx + ngx - k, ngx)], tot_x.at[lax.rem(gx + ngx - k, ngx)], sx.at[k], rx.at[k],
               (lax.rem(gx + k, ngx), gy))
        for k in range(1, ngx)
    ]
    for c in incoming:
        c.wait_recv()
    mine = tot_x[0]
    for k in range(1, ngx):
        mine = mine + tot_x[k]
    whole = jnp.broadcast_to(jnp.sum(mine, axis=1, keepdims=True), (2 * M, TILE))
    r8, l8 = iota((2 * M, TILE), 0), iota((2 * M, TILE), 1)
    for n in range(2):
        line = jnp.sum(jnp.where(r8 == 2 * l8 + n, whole, 0.0), axis=0, keepdims=True)
        totals[n : n + 1, :] = line[:, 0:M]

    for c in tile_copies + copies + copies_x:
        c.wait_send()
    for (dx, dy), c in disp_moves:
        @pl.when(exists(dx, dy))
        def _(c=c):
            c.wait_send()
    for dx, dy, c in halo:
        @pl.when(exists(dx, dy))
        def _(c=c):
            c.wait_send()


def local(ngx, ngy, density, energy, displacement, tile_mat, store_frac, store_state, store_route):
    rows, width = density.shape
    cap = rows * (width // TILE) // 16
    ext, full = width + TILE, rows + 16
    wide = -(-max(3 * TILE, ngy * cap) // TILE) * TILE
    vmem, dma = pltpu.VMEM, pltpu.SemaphoreType.DMA
    spec = pl.BlockSpec(memory_space=pltpu.VMEM)
    far = pl.BlockSpec(memory_space=pltpu.HBM)
    inputs = (density, energy, displacement, tile_mat.T, store_frac, store_state, store_route)
    scratch = [
        *(vmem(x.shape, x.dtype) for x in inputs),
        dma((7,)),
        vmem((rows * (width // TILE), TILE), f32),
        vmem((ngy, cap + 8, wide), f32),
        vmem((ngy, cap + 8, wide), f32),
        vmem((8, width), f32),
        vmem((8, width), f32),
        vmem((rows, TILE), f32),
        vmem((rows + 8, TILE), f32),
        vmem((2, rows + 8, ext), f32),
        vmem((rows + 8, ext), f32),
        vmem((rows + 8, ext), f32),
        vmem((rows, ext), f32),
        vmem((rows, ext), f32),
        vmem((F, full, ext), f32),
        vmem((rows, TILE), f32),
        vmem((2, 2 * F, width), f32),
        vmem((2, full, TILE), f32),
        vmem((2, 2 * F, width), f32),
        vmem((F, 8, TILE), f32),
        vmem((ngy, 2 * M, TILE), f32),
        vmem((ngx, 2 * M, TILE), f32),
        vmem((8, TILE), f32),
        dma((ngy,)), dma((ngy,)), dma((8,)), dma((8,)), dma((3,)), dma((3,)),
        dma((ngy,)), dma((ngy,)), dma((ngx,)), dma((ngx,)),
    ]
    remapped, totals = pl.pallas_call(
        functools.partial(kernel, ngx, ngy, cap),
        out_shape=(pltpu.VMEM((F, rows, width), f32), jax.ShapeDtypeStruct((2, M), f32)),
        in_specs=[far] * 7,
        out_specs=(spec, spec),
        scratch_shapes=scratch,
        compiler_params=pltpu.CompilerParams(
            collective_id=0, has_side_effects=True, vmem_limit_bytes=61 * 1024 * 1024
        ),
    )(*inputs)
    return remapped.reshape(M, 3, rows, width), totals


def solution(mesh):
    placed = (
        P("gx", "gy"),
        P("gx", "gy"),
        P(None, "gx", "gy"),
        P("gx", "gy"),
        P(("gx", "gy"), None),
        P(None, ("gx", "gy"), None),
        P(None, ("gx", "gy")),
    )
    return jax.shard_map(
        functools.partial(local, mesh.shape["gx"], mesh.shape["gy"]),
        mesh=mesh,
        in_specs=placed,
        out_specs=(P(None, None, "gx", "gy"), P()),
        check_vma=False,
    )
```

```python
import functools
import jax
import jax.numpy as jnp
from jax import lax
from jax.experimental import pallas as pl
from jax.experimental.pallas import tpu as pltpu
from jax.sharding import PartitionSpec as P

M = 4
F = 3 * M
TILE = 128
MESH = pl.DeviceIdType.MESH
f32 = jnp.float32
bf16 = jnp.bfloat16
NT = (((1,), (1,)), ((), ()))


def iota(shape, dim):
    return lax.broadcasted_iota(jnp.int32, shape, dim)


def split2(x):
    hi = x.astype(bf16)
    rest = x - hi.astype(f32)
    return hi, rest.astype(bf16)


def pick(onehot, data):
    parts = split2(data)
    o = onehot.astype(bf16)
    low = jnp.dot(o, parts[1], preferred_element_type=f32)
    return low + jnp.dot(o, parts[0], preferred_element_type=f32)


def kernel(
    ngx, ngy, cap,
    density_h, energy_h, disp_h, mat_h, frac_h, state_h, route_h,
    out, totals,
    density, energy, disp, mat, frac, state, route, s0,
    primary, send1, got1, drow, drow_in, dcol, dcol_in, de, ax, bx, ay, by,
    q, pk, xs, cols_in, rows_in, part, tot_y, tot_x, tot_sum,
    s1, r1, s2, r2, s3, r3, sy, ry, sx, rx,
):
    gx, gy = lax.axis_index("gx"), lax.axis_index("gy")
    rows, width = density.shape
    ext = width + TILE
    full = rows + 16
    per_row = width // TILE
    slots = frac.shape[0]
    up, down = gx > 0, gx < ngx - 1
    left, right = gy > 0, gy < ngy - 1

    def exists(dx, dy):
        ok = True
        if dx:
            ok = up if dx < 0 else down
        if dy:
            side = left if dy < 0 else right
            ok = side if ok is True else jnp.logical_and(ok, side)
        return ok

    loads = [
        pltpu.make_async_copy(src, dst, s0.at[n])
        for n, (src, dst) in enumerate(
            (
                (route_h, route), (frac_h, frac), (state_h, state), (disp_h, disp),
                (mat_h, mat), (density_h, density), (energy_h, energy),
            )
        )
    ]
    for c in loads[:3]:
        c.start()

    barrier = pltpu.get_barrier_semaphore()
    diagonals = [(-1, -1), (-1, 1), (1, -1), (1, 1)]
    for k in range(1, ngy):
        pl.semaphore_signal(barrier, inc=1, device_id=(gx, lax.rem(gy + k, ngy)), device_id_type=MESH)
    for k in range(1, ngx):
        pl.semaphore_signal(barrier, inc=1, device_id=(lax.rem(gx + k, ngx), gy), device_id_type=MESH)
    for dx, dy in diagonals:
        @pl.when(exists(dx, dy))
        def _(dx=dx, dy=dy):
            pl.semaphore_signal(barrier, inc=1, device_id=(gx + dx, gy + dy), device_id_type=MESH)

    for c in loads[3:]:
        c.start()

    count = ngy * cap
    loads[0].wait()
    target = route[0:1, :]
    row = iota((count, slots), 0)
    wanted = lax.rem(gy + row // cap, ngy)
    member = (jnp.broadcast_to(target, (count, slots)) == wanted).astype(f32)
    before = (iota((slots, slots), 0) < iota((slots, slots), 1)).astype(bf16)
    rank = jnp.dot(member.astype(bf16), before, preferred_element_type=f32)
    chosen = jnp.where(rank == (row % cap).astype(f32), member, 0.0)
    loads[1].wait()
    loads[2].wait()
    payload = jnp.concatenate([frac[...], state[0], state[1]], axis=1)
    packed = pick(chosen, payload)
    named = jnp.concatenate(
        [
            ((route[1:2, :] + 1) // 128).astype(f32), (route[2:3, :] + 1).astype(f32),
            ((route[1:2, :] + 1) % 128).astype(f32), jnp.zeros((5, slots), f32),
        ],
        axis=0,
    )
    labels = lax.dot_general(named.astype(bf16), chosen.astype(bf16), NT, preferred_element_type=f32)
    label_lane = iota((8, count), 1) // cap
    wide = send1.shape[2]
    for k in range(ngy):
        dst = got1 if k == 0 else send1
        dst[k, 0:cap, 0 : 3 * TILE] = packed[k * cap : (k + 1) * cap]
        dst[k, cap : cap + 8, 0:count] = jnp.where(label_lane == k, labels, 0.0)

    loads[3].wait()
    drow[...] = jnp.concatenate([disp[0, 0:8][0:1], disp[1, 0:8][0:1], jnp.zeros((6, width), f32)], axis=0)
    lane_r = iota((rows, TILE), 1)
    dcol[...] = jnp.where(lane_r == 0, disp[0, :, 0:TILE], pltpu.roll(disp[1, :, 0:TILE], 1, 1))

    diag_count = sum(exists(dx, dy).astype(jnp.int32) for dx, dy in diagonals)
    pl.semaphore_wait(barrier, ngy - 1 + ngx - 1 + diag_count)

    def remote(src, dst, s, r, to):
        return pltpu.make_async_remote_copy(
            src_ref=src, dst_ref=dst, send_sem=s, recv_sem=r, device_id=to, device_id_type=MESH
        )

    tile_copies = [
        remote(send1.at[k], got1.at[k], s1.at[k], r1.at[k], (gx, lax.rem(gy + k, ngy)))
        for k in range(1, ngy)
    ]
    for c in tile_copies:
        c.start()
    disp_moves = [
        ((-1, 0), remote(drow, drow_in, s3.at[0], r3.at[0], (gx - 1, gy))),
        ((0, -1), remote(dcol, dcol_in.at[0:rows], s3.at[1], r3.at[1], (gx, gy - 1))),
        ((-1, -1), remote(dcol.at[0:8], dcol_in.at[rows : rows + 8], s3.at[2], r3.at[2], (gx - 1, gy - 1))),
    ]
    for (dx, dy), c in disp_moves:
        @pl.when(exists(dx, dy))
        def _(c=c):
            c.start()

    @pl.when(jnp.logical_not(down))
    def _():
        drow_in[...] = jnp.zeros(drow_in.shape, f32)

    @pl.when(jnp.logical_not(right))
    def _():
        dcol_in[0:rows] = jnp.zeros((rows, TILE), f32)

    @pl.when(jnp.logical_not(exists(1, 1)))
    def _():
        dcol_in[rows : rows + 8] = jnp.zeros((8, TILE), f32)

    def row_span(dx):
        return {1: slice(0, 8), 0: slice(8, 8 + rows), -1: slice(8 + rows, full)}[dx]

    def col_span(dx):
        return {1: slice(rows - 8, rows), 0: slice(0, rows), -1: slice(0, 8)}[dx]

    def halo_copy(n, dx, dy):
        to = (gx + dx, gy + dy)
        if dy == 0:
            src, dst = xs.at[1 if dx > 0 else 0], rows_in.at[0 if dx > 0 else 1]
        else:
            src = pk.at[col_span(dx)]
            dst = cols_in.at[0 if dy > 0 else 1, row_span(dx)]
        return remote(src, dst, s2.at[n], r2.at[n], to)

    directions = [(0, 1), (0, -1)] + diagonals + [(1, 0), (-1, 0)]
    halo = [(dx, dy, halo_copy(n, dx, dy)) for n, (dx, dy) in enumerate(directions)]
    for dx, dy, _c in halo:
        @pl.when(jnp.logical_not(exists(-dx, -dy)))
        def _(dx=dx, dy=dy):
            if dy == 0:
                rows_in[0 if dx > 0 else 1] = jnp.zeros(rows_in.shape[1:], f32)
            else:
                span = row_span(dx)
                cols_in[0 if dy > 0 else 1, span] = jnp.zeros((span.stop - span.start, TILE), f32)

    zero8 = jnp.zeros((8, ext), f32)
    for f in range(F):
        q[f, 0:8] = zero8
        q[f, full - 8 : full] = zero8

    for c in loads[4:]:
        c.wait()
    eye = iota((rows, rows), 0) == iota((rows, rows), 1)
    spread = jnp.concatenate(
        [jnp.where(eye, mat[c : c + 1, :].astype(f32), 0.0).astype(bf16) for c in range(per_row)], axis=0
    )
    primary[...] = jnp.dot(spread, jnp.ones((rows, TILE), bf16), preferred_element_type=f32)

    for c in tile_copies:
        c.wait_recv()
    label = got1[0, cap : cap + 8, 0:count]
    for k in range(1, ngy):
        label = label + got1[k, cap : cap + 8, 0:count]
    tiles = per_row * rows
    place = iota((tiles, count), 0)
    place = (place % rows) * per_row + place // rows + 1
    tile_at = (label[0:1, :] * 128.0 + label[2:3, :]).astype(jnp.int32)
    hit = (jnp.broadcast_to(tile_at, (tiles, count)) == place).astype(f32)
    arrived = jnp.concatenate([got1[k, 0:cap, 0 : 3 * TILE] for k in range(ngy)], axis=0)
    mixed = pick(hit, arrived)
    second = jnp.dot(
        (hit * label[1:2, :]).astype(bf16), jnp.ones((count, TILE), bf16), preferred_element_type=f32
    )
    edge = []
    for c in [0] + list(range(per_row - 1, 0, -1)):
        at = slice(c * rows, (c + 1) * rows)
        lanes = slice(c * TILE, (c + 1) * TILE)
        fr, d2, e2 = (mixed[at, n * TILE : (n + 1) * TILE] for n in range(3))
        other_m = second[at]
        own_m = primary[at]
        d1 = density[:, lanes]
        e1 = energy[:, lanes]
        de1 = d1 * e1
        de2 = d2 * e2
        clear = 1.0 - fr
        for m in range(M):
            own = jnp.where(own_m == float(m), clear, 0.0)
            oth = jnp.where(other_m == m + 1.0, fr, 0.0)
            for n, value in enumerate((own + oth, own * d1 + oth * d2, own * de1 + oth * de2)):
                q[3 * m + n, 8 : 8 + rows, lanes] = value
    for f in range(F):
        xs[0, 2 * f : 2 * f + 2] = q[f, 8:16, 0:width][0:2]
        xs[1, 2 * f : 2 * f + 2] = q[f, rows : rows + 8, 0:width][6:8]
    for dx, dy, c in halo[6:]:
        @pl.when(exists(dx, dy))
        def _(c=c):
            c.start()
    acc = jnp.zeros((rows, TILE), f32)
    for f in range(F):
        both = jnp.where(
            lane_r < TILE // 2, q[f, 8 : 8 + rows, 0:TILE], q[f, 8 : 8 + rows, width - TILE : width]
        )
        acc = jnp.where(lane_r // 4 == f, pltpu.roll(both, 4 * f + 2, 1), acc)
    pk[...] = acc
    for dx, dy, c in halo[:6]:
        @pl.when(exists(dx, dy))
        def _(c=c):
            c.start()

    for (dx, dy), c in disp_moves:
        @pl.when(exists(-dx, -dy))
        def _(c=c):
            c.wait_recv()
    dc = dcol_in[...]
    for c in range(2):
        de[c, 0:rows, 0:width] = disp[c]
        de[c, rows : rows + 8, 0:width] = jnp.broadcast_to(drow_in[c : c + 1, :], (8, width))
        de[c, :, width:ext] = dc if c == 0 else pltpu.roll(dc, TILE - 1, 1)
    face = iota((rows + 8, ext), 0)
    closed_x = jnp.logical_or(
        jnp.logical_and(face == 0, jnp.logical_not(up)), jnp.logical_and(face == rows, jnp.logical_not(down))
    )
    d0 = de[0]
    speed = jnp.where(closed_x, 0.0, -0.5 * (d0 + pltpu.roll(d0, ext - 1, 1)))
    ax[...] = jnp.maximum(speed, 0.0)
    bx[...] = jnp.minimum(speed, 0.0)
    face = iota((rows, ext), 1)
    closed_y = jnp.logical_or(
        jnp.logical_and(face == 0, jnp.logical_not(left)), jnp.logical_and(face == width, jnp.logical_not(right))
    )
    d1 = de[1]
    speed = jnp.where(closed_y, 0.0, -0.5 * (d1[0:rows] + pltpu.roll(d1, rows + 7, 0)[0:rows]))
    ay[...] = jnp.maximum(speed, 0.0)
    by[...] = jnp.minimum(speed, 0.0)

    for dx, dy, c in halo:
        @pl.when(exists(-dx, -dy))
        def _(c=c):
            c.wait_recv()
    lane_f = iota((full, TILE), 1)
    ring = jnp.where(lane_f % 4 < 2, cols_in[0], cols_in[1])
    for f in range(F):
        q[f, :, width:ext] = pltpu.roll(ring, TILE - 4 * f - 2, 1)
        q[f, 6:8, 0:width] = rows_in[0, 2 * f : 2 * f + 2]
        q[f, 8 + rows : 10 + rows, 0:width] = rows_in[1, 2 * f : 2 * f + 2]

    blocks = full // 8
    sub = iota((8, ext), 0)
    twelfth = 1.0 / 12.0

    def one_field(f, carry):
        qs, sums, diffs, hs, fluxes = {}, {}, {}, {}, {}

        def load(b):
            if b not in qs:
                v = q[f, b * 8 : b * 8 + 8]
                before, after = pltpu.roll(v, 1, 1), pltpu.roll(v, ext - 1, 1)
                qs[b], sums[b], diffs[b] = v, v + before + after, after - before

        def prev(values, b):
            if b == 0:
                return pltpu.roll(values[b], 1, 0)
            return pltpu.roll(jnp.where(sub == 7, values[b - 1], values[b]), 1, 0)

        def follow(values, b):
            if b == blocks - 1:
                return pltpu.roll(values[b], 7, 0)
            return pltpu.roll(jnp.where(sub == 0, values[b + 1], values[b]), 7, 0)

        low, high = {}, {}

        def sides(b):
            if b not in low:
                for n in (b - 1, b, b + 1):
                    if 0 <= n < blocks:
                        load(n)
                h = (follow(sums, b) - prev(sums, b)) * twelfth
                low[b], high[b] = qs[b] + h, qs[b] - h

        def flux(b):
            if b not in fluxes:
                sides(b - 1)
                sides(b)
                at = slice(b * 8 - 8, b * 8)
                fluxes[b] = ax[at] * prev(low, b) + bx[at] * high[b]

        total = jnp.zeros((8, width), f32)
        for b in range(1, blocks - 1):
            flux(b)
            flux(b + 1)
            at = slice(b * 8 - 8, b * 8)
            h = (diffs[b] + prev(diffs, b) + follow(diffs, b)) * twelfth
            fy = ay[at] * pltpu.roll(qs[b] + h, 1, 1) + by[at] * (qs[b] - h)
            value = qs[b] + fluxes[b] - follow(fluxes, b) + fy - pltpu.roll(fy, ext - 1, 1)
            value = value[:, 0:width]
            out[f, at] = value
            total = total + value
        lanes = total[:, 0:TILE]
        for c in range(1, per_row):
            lanes = lanes + total[:, c * TILE : (c + 1) * TILE]
        part[f] = lanes
        return carry

    def volumes(first, last):
        lax.fori_loop(first, last, lambda m, carry: one_field(3 * m, carry), 0)

    lax.fori_loop(0, 2 * M, lambda n, carry: one_field(n + n // 2 + 1, carry), 0)

    mine = jnp.concatenate(
        [jnp.sum(part[3 * m + n], axis=0, keepdims=True) for m in range(M) for n in (1, 2)], axis=0
    )
    tot_y[gy] = mine
    copies = [
        remote(tot_y.at[gy], tot_y.at[gy], sy.at[k], ry.at[k], (gx, lax.rem(gy + k, ngy)))
        for k in range(1, ngy)
    ]
    for c in copies:
        c.start()
    volumes(0, M // 2)
    incoming = [
        remote(tot_y.at[lax.rem(gy + ngy - k, ngy)], tot_y.at[lax.rem(gy + ngy - k, ngy)], sy.at[k], ry.at[k],
               (gx, lax.rem(gy + k, ngy)))
        for k in range(1, ngy)
    ]
    for c in incoming:
        c.wait_recv()
    mine = tot_y[0]
    for k in range(1, ngy):
        mine = mine + tot_y[k]
    tot_x[gx] = mine
    copies_x = [
        remote(tot_x.at[gx], tot_x.at[gx], sx.at[k], rx.at[k], (lax.rem(gx + k, ngx), gy))
        for k in range(1, ngx)
    ]
    for c in copies_x:
        c.start()
    volumes(M // 2, M)
    incoming = [
        remote(tot_x.at[lax.rem(gx + ngx - k, ngx)], tot_x.at[lax.rem(gx + ngx - k, ngx)], sx.at[k], rx.at[k],
               (lax.rem(gx + k, ngx), gy))
        for k in range(1, ngx)
    ]
    for c in incoming:
        c.wait_recv()
    mine = tot_x[0]
    for k in range(1, ngx):
        mine = mine + tot_x[k]
    whole = jnp.broadcast_to(jnp.sum(mine, axis=1, keepdims=True), (2 * M, TILE))
    r8, l8 = iota((2 * M, TILE), 0), iota((2 * M, TILE), 1)
    for n in range(2):
        line = jnp.sum(jnp.where(r8 == 2 * l8 + n, whole, 0.0), axis=0, keepdims=True)
        totals[n : n + 1, :] = line[:, 0:M]

    for c in tile_copies + copies + copies_x:
        c.wait_send()
    for (dx, dy), c in disp_moves:
        @pl.when(exists(dx, dy))
        def _(c=c):
            c.wait_send()
    for dx, dy, c in halo:
        @pl.when(exists(dx, dy))
        def _(c=c):
            c.wait_send()


def local(ngx, ngy, density, energy, displacement, tile_mat, store_frac, store_state, store_route):
    rows, width = density.shape
    cap = rows * (width // TILE) // 16
    ext, full = width + TILE, rows + 16
    wide = -(-max(3 * TILE, ngy * cap) // TILE) * TILE
    vmem, dma = pltpu.VMEM, pltpu.SemaphoreType.DMA
    spec = pl.BlockSpec(memory_space=pltpu.VMEM)
    far = pl.BlockSpec(memory_space=pltpu.HBM)
    inputs = (density, energy, displacement, tile_mat.T, store_frac, store_state, store_route)
    scratch = [
        *(vmem(x.shape, x.dtype) for x in inputs),
        dma((7,)),
        vmem((rows * (width // TILE), TILE), f32),
        vmem((ngy, cap + 8, wide), f32),
        vmem((ngy, cap + 8, wide), f32),
        vmem((8, width), f32),
        vmem((8, width), f32),
        vmem((rows, TILE), f32),
        vmem((rows + 8, TILE), f32),
        vmem((2, rows + 8, ext), f32),
        vmem((rows + 8, ext), f32),
        vmem((rows + 8, ext), f32),
        vmem((rows, ext), f32),
        vmem((rows, ext), f32),
        vmem((F, full, ext), f32),
        vmem((rows, TILE), f32),
        vmem((2, 2 * F, width), f32),
        vmem((2, full, TILE), f32),
        vmem((2, 2 * F, width), f32),
        vmem((F, 8, TILE), f32),
        vmem((ngy, 2 * M, TILE), f32),
        vmem((ngx, 2 * M, TILE), f32),
        vmem((8, TILE), f32),
        dma((ngy,)), dma((ngy,)), dma((8,)), dma((8,)), dma((3,)), dma((3,)),
        dma((ngy,)), dma((ngy,)), dma((ngx,)), dma((ngx,)),
    ]
    remapped, totals = pl.pallas_call(
        functools.partial(kernel, ngx, ngy, cap),
        out_shape=(pltpu.VMEM((F, rows, width), f32), jax.ShapeDtypeStruct((2, M), f32)),
        in_specs=[far] * 7,
        out_specs=(spec, spec),
        scratch_shapes=scratch,
        compiler_params=pltpu.CompilerParams(
            collective_id=0, has_side_effects=True, vmem_limit_bytes=61 * 1024 * 1024
        ),
    )(*inputs)
    return remapped.reshape(M, 3, rows, width), totals


def solution(mesh):
    placed = (
        P("gx", "gy"),
        P("gx", "gy"),
        P(None, "gx", "gy"),
        P("gx", "gy"),
        P(("gx", "gy"), None),
        P(None, ("gx", "gy"), None),
        P(None, ("gx", "gy")),
    )
    return jax.shard_map(
        functools.partial(local, mesh.shape["gx"], mesh.shape["gy"]),
        mesh=mesh,
        in_specs=placed,
        out_specs=(P(None, None, "gx", "gy"), P()),
        check_vma=False,
    )
```
